128 devices in a mesh: band: 8 (over y, core), lev: 16 (over z, x).
Axes of the slice: x: 4, y: 4, z: 4, core: 2. Of those that a mesh axis runs over, the one named last changes fastest.
Arguments:
- grid_values: bfloat16 [1024, 2, 128, 3072], P(('band', 'lev')), may hold values from -6 to 6
- lon_counts: int32 [1024], P(('band', 'lev')), may hold values from 1536 to 3072, as said below
- legendre: bfloat16 [768, 2, 1024, 384], P('lev', None, 'band'), as said below
Outputs:
- spectra: float32 [768, 2, 2, 128, 384], P('lev', None, None, 'band')
The draws below stay inside these ranges and needn't reach their ends.
Inputs may be any that keep to these rules, and one draw needn't show every extreme that they name: `lon_counts`: A multiple of 4 for every pair, equal to 3072 for some pair. legendre[m, s, p, i] is zero where m + 2 i + s >= 768.
All inputs are finite; a program needn't handle non-finite values.
Results may differ from the reference program's by a relative error of at most 0.015.
Values may be sent and summed in bfloat16 or wider, within the bound.
A program may use at most 128 MiB of HBM per device.

```python
import math
import jax
import jax.numpy as jnp
from jax import lax

NLON = 3072
TM = 768
FLD = 128
NLATP = 1024
N_BAND = 8


def draw_lon_counts(key, part):
    reductions = jax.random.randint(key, (NLATP,), 0, NLON // 8 + 1, dtype=jnp.int32)
    counts = NLON - 4 * reductions
    return counts.at[0].set(NLON)


def draw_legendre(key, part):
    wavenumbers = jnp.arange(TM, dtype=jnp.int32)[:, None, None, None]
    parities = jnp.arange(2, dtype=jnp.int32)[None, :, None, None]
    indices = jnp.arange(TM // 2, dtype=jnp.int32)[None, None, None, :]
    keep = (wavenumbers + 2 * indices + parities < TM).astype(jnp.float32)
    spread = 0.87 * (NLON / NLATP) ** 0.5
    values = jax.random.normal(key, (TM, 2, NLATP, TM // 2), jnp.float32)
    return (values * spread * keep).astype(jnp.bfloat16)


def block_scale(own_key, extent, pieces, smallest, largest):
    level = 1.0
    for axis_at, blocks in pieces:
        draws = jax.random.uniform(jax.random.fold_in(jax.random.fold_in(own_key, 6), axis_at), (blocks,), jnp.float32, smallest / len(pieces), largest / len(pieces))
        level = level * jnp.repeat(jnp.exp(draws), extent[axis_at] // blocks).reshape((-1,) + (1,) * (len(extent) - 1 - axis_at))
    return level


def gaussian(stream_key, extent, width, bound, pieces=(), held_as=jnp.bfloat16):
    entries = width * jax.random.normal(stream_key, extent, jnp.float32)
    if pieces:
        entries = entries * block_scale(stream_key, extent, pieces, -0.22, 0.18)
    return jnp.clip(entries, -bound, bound).astype(held_as)


def setup_inputs(seed: int = 0) -> dict:
    key_list = jax.random.split(jax.random.key(seed), 4)
    grid_values = gaussian(key_list[0], (NLATP, 2, FLD, NLON), 1.0, 6.0, ((0, 128),))
    lon_counts = draw_lon_counts(jax.random.fold_in(key_list[3], 71), 0)
    legendre = draw_legendre(jax.random.fold_in(key_list[3], 71), 0)
    return {"grid_values": grid_values, "lon_counts": lon_counts, "legendre": legendre}


def fourier_table(lon_count, points, orders):
    positions = jnp.arange(points, dtype=jnp.int32)
    wavenumbers = jnp.arange(orders, dtype=jnp.int32)
    residues = (wavenumbers[:, None] * positions[None, :]) % lon_count
    scale_back = 1.0 / lon_count.astype(jnp.float32)
    angles = residues.astype(jnp.float32) * (2.0 * math.pi * scale_back)
    inside = (positions < lon_count)[None, :]
    cosines = jnp.where(inside, jnp.cos(angles) * scale_back, 0.0)
    sines = jnp.where(inside, -jnp.sin(angles) * scale_back, 0.0)
    return jnp.stack([cosines, sines], axis=1).astype(jnp.bfloat16)


def reference(grid_values, lon_counts, legendre):
    pairs = grid_values.shape[0]
    fields = grid_values.shape[2]
    points = grid_values.shape[3]
    orders = legendre.shape[0]
    half_orders = legendre.shape[3]
    group_pairs = pairs // N_BAND

    def pair_fourier(inputs):
        lat_rows, lon_count = inputs
        wave_table = fourier_table(lon_count, points, orders)
        return jnp.einsum("mrj,hfj->mrhf", wave_table.astype(jnp.float32), lat_rows.astype(jnp.float32))

    def add_group(group, summed):
        first_pair = (group * group_pairs).astype(jnp.int32)
        lat_rows = lax.dynamic_slice_in_dim(grid_values, first_pair, group_pairs, 0)
        counts_here = lax.dynamic_slice_in_dim(lon_counts, first_pair, group_pairs, 0)
        fourier = lax.map(pair_fourier, (lat_rows, counts_here))
        north = fourier[:, :, :, 0, :]
        south = fourier[:, :, :, 1, :]
        folded = jnp.stack([north + south, north - south]).astype(jnp.bfloat16)
        weights = lax.dynamic_slice_in_dim(legendre, first_pair, group_pairs, 2)
        partial_sums = jnp.einsum("spmrf,mspi->msrfi", folded.astype(jnp.float32), weights.astype(jnp.float32))
        rounded = lax.optimization_barrier(partial_sums.astype(jnp.bfloat16))
        return summed + rounded.astype(jnp.float32)

    initial = jnp.zeros((orders, 2, 2, fields, half_orders), jnp.float32)
    return lax.fori_loop(0, N_BAND, add_group, initial)
```

```python
import functools

import jax
import jax.numpy as jnp
from jax import lax
from jax.experimental import pallas as pl
from jax.experimental.pallas import tpu as pltpu
from jax.sharding import PartitionSpec as P

F32 = jnp.float32
BF16 = jnp.bfloat16
COS = (1.0, -19.73920440673828, 64.9390869140625, -85.4496078491211, 60.16310119628906, -25.950063705444336, 6.50340461730957)
SIN = (6.283182621002197, -41.341392517089844, 81.59541320800781, -76.57229614257812, 41.17121124267578, -12.217327117919922)
LANES = 128


def poly(coefs, z):
    out = jnp.full_like(z, coefs[-1])
    for coef in coefs[-2::-1]:
        out = out * z + coef
    return out


def cos_sin(products, count, inverse):
    turns = jnp.floor(products * inverse + 0.5)
    t = (products - turns * count) * inverse
    z = t * t
    return poly(COS, z), t * poly(SIN, z)


def prepare_kernel(owners, owned, counts_ref, inverse_ref, x_ref, y_ref, coarse_ref, fine_ref):
    pair = pl.program_id(0)
    count = counts_ref[pair]
    quarter = lax.shift_right_logical(count, 2)
    fields, points = x_ref.shape[1:]
    width = points // 4
    tiles = width // LANES
    last = points - width - LANES
    rows = 16
    lane = lax.broadcasted_iota(jnp.int32, (rows, LANES), 1)
    starts, shifts = [], []
    for k in range(4):
        start = jnp.minimum(quarter * k // LANES * LANES, last)
        starts.append(start)
        shifts.append(quarter * k - start)

    def fold(step, carry):
        row = pl.ds(pl.multiple_of(step * rows, rows), rows)
        pieces = []
        for k in range(4):
            shift = shifts[k]
            both = []
            for h in range(2):
                turned = []
                for i in range(tiles + (k > 0)):
                    at = pl.multiple_of(starts[k] + i * LANES, LANES)
                    v = x_ref[h, row, pl.ds(at, LANES)].astype(F32)
                    if k:
                        v = pltpu.roll(v, (LANES - shift) & (LANES - 1), 1)
                    turned.append(v)
                if k:
                    keep = lane < LANES - shift
                    turned = [jnp.where(keep, turned[i], turned[i + 1]) for i in range(tiles)]
                both.append(turned)
            pieces.append([[n + s for n, s in zip(*both)], [n - s for n, s in zip(*both)]])
        for s in range(2):
            to = pl.ds(pl.multiple_of(step * rows + s * fields, rows), rows)
            for i in range(tiles):
                inside = lane + i * LANES < quarter
                x0, x1, x2, x3 = (jnp.where(inside, pieces[k][s][i], 0.0) for k in range(4))
                at = pl.ds(i * LANES, LANES)
                y_ref[0, to, at] = ((x0 + x2) + (x1 + x3)).astype(BF16)
                y_ref[1, to, at] = (x0 - x2).astype(BF16)
                y_ref[2, to, at] = ((x0 + x2) - (x1 + x3)).astype(BF16)
                y_ref[3, to, at] = (x1 - x3).astype(BF16)
        return carry

    lax.fori_loop(0, fields // rows, fold, 0)

    n = count.astype(F32)
    inverse = inverse_ref[pair]
    groups = owned // 4
    middle = 2 * groups - 2
    place = lax.broadcasted_iota(jnp.int32, (16, width), 1).astype(F32)
    row = lax.broadcasted_iota(jnp.int32, (16, width), 0).astype(F32)
    for step in range(groups // 2):
        c, s = cos_sin(place * float(4 * step + 2), n, inverse)
        fine_ref[step, 0] = c.astype(BF16)
        fine_ref[step, 1] = s.astype(BF16)
    owner_cos, owner_sin = cos_sin(place * (row * float(owned)), n, inverse)
    owner_cos, owner_sin = owner_cos * inverse, owner_sin * inverse
    for u in range(4):
        c, s = cos_sin(place * float(middle + u), n, inverse)
        coarse_ref[u, 0] = (owner_cos * c - owner_sin * s).astype(BF16)
        coarse_ref[u, 1] = (owner_sin * c + owner_cos * s).astype(BF16)


def prepare(grid_values, lon_counts, owners, owned):
    pairs, _, fields, points = grid_values.shape
    width = points // 4
    halves = owned // 8
    smem = pl.BlockSpec(memory_space=pltpu.SMEM)
    return pl.pallas_call(
        functools.partial(prepare_kernel, owners, owned),
        grid=(pairs,),
        out_shape=(
            jax.ShapeDtypeStruct((pairs, 4, 2 * fields, width), BF16),
            jax.ShapeDtypeStruct((pairs, 4, 2, owners, width), BF16),
            jax.ShapeDtypeStruct((pairs, halves, 2, owners, width), BF16),
        ),
        in_specs=[smem, smem, pl.BlockSpec((None, 2, fields, points), lambda p: (p, 0, 0, 0))],
        out_specs=(
            pl.BlockSpec((None, 4, 2 * fields, width), lambda p: (p, 0, 0, 0)),
            pl.BlockSpec((None, 4, 2, owners, width), lambda p: (p, 0, 0, 0, 0)),
            pl.BlockSpec((None, halves, 2, owners, width), lambda p: (p, 0, 0, 0, 0)),
        ),
        compiler_params=pltpu.CompilerParams(vmem_limit_bytes=48 * 2**20),
    )(lon_counts, 1.0 / lon_counts.astype(F32), grid_values)


def transform_kernel(u, *refs):
    if u % 2:
        a_ref, b_ref, coarse_ref, fine_ref, out_ref, table, total = refs
        sources = (a_ref, b_ref)
    else:
        a_ref, coarse_ref, fine_ref, out_ref, table, total = refs
        sources = (a_ref,)
    pair = pl.program_id(0)
    pairs = pl.num_programs(0)
    halves = fine_ref.shape[0]
    owners = coarse_ref.shape[1]
    for step in range(halves):
        for j, (k, l) in enumerate(((0, 0), (1, 0), (0, 1), (1, 1))):
            table[pl.ds((4 * step + j) * owners, owners), :] = coarse_ref[k] * fine_ref[step, l]
    sums = [
        lax.dot_general(table[...], ref[...], (((1,), (1,)), ((), ())), preferred_element_type=F32)
        for ref in sources
    ]
    spot = pl.ds(pair, owners, stride=8)
    fields = out_ref.shape[-1]

    def keep(t, real, imag):
        for r, value in enumerate((real, imag)):
            for s in range(2):
                total[4 * t + 2 * r + s, spot, :] = value[:, s * fields : (s + 1) * fields]

    for step in range(halves):
        waves = []
        for part in sums:
            cc, sc, cs, ss = (part[(4 * step + j) * owners : (4 * step + j + 1) * owners] for j in range(4))
            waves.append((cc - ss, sc + cs, cc + ss, sc - cs))
        if u % 2:
            (ca, sa, da, ta), (cb, sb, db, tb) = waves
            if u == 1:
                keep(halves + step, ca - sb, -(sa + cb))
                keep(halves - 1 - step, da - tb, -(ta + db))
            else:
                keep(halves + step, ca + sb, cb - sa)
                keep(halves - 1 - step, da + tb, db - ta)
        else:
            ((ca, sa, da, ta),) = waves
            keep(halves + step, ca, -sa)
            keep(halves - 1 - step, da, -ta)

    @pl.when(pair == pairs - 1)
    def _():
        for t in range(2 * halves):
            for s in range(2):
                real = total[4 * t + s].reshape(owners, 8, fields)
                imag = total[4 * t + 2 + s].reshape(owners, 8, fields)
                out_ref[:, t, s] = jnp.concatenate([real, imag], axis=1).astype(BF16)


def transform(u, y, coarse, fine):
    pairs, _, columns, width = y.shape
    halves, _, owners = fine.shape[1:4]
    fields = columns // 2
    used = (1, 3) if u % 2 else (u,)
    return pl.pallas_call(
        functools.partial(transform_kernel, u),
        grid=(pairs,),
        out_shape=jax.ShapeDtypeStruct((owners, 2 * halves, 2, 2 * pairs, fields), BF16),
        in_specs=[pl.BlockSpec((None, None, columns, width), functools.partial(lambda k, p: (p, k, 0, 0), k)) for k in used]
        + [
            pl.BlockSpec((None, None, 2, owners, width), lambda p: (p, u, 0, 0, 0)),
            pl.BlockSpec((None, halves, 2, owners, width), lambda p: (p, 0, 0, 0, 0)),
        ],
        out_specs=pl.BlockSpec((owners, 2 * halves, 2, 2 * pairs, fields), lambda p: (0, 0, 0, 0, 0)),
        scratch_shapes=[
            pltpu.VMEM((4 * halves * owners, width), BF16),
            pltpu.VMEM((8 * halves, owners * pairs, fields), F32),
        ],
        compiler_params=pltpu.CompilerParams(vmem_limit_bytes=48 * 2**20),
    )(*[y] * len(used), coarse, fine)


def legendre_kernel(f_ref, l_ref, out_ref):
    owners, _, both, fields = f_ref.shape
    pairs = both // 2
    for s in range(2):
        f = f_ref[:, s].astype(F32).reshape(owners, 2, pairs, fields)
        for r in range(2):
            part = f[:, r].reshape(owners * pairs, fields).astype(BF16)
            out_ref[s, r] = lax.dot_general(
                part, l_ref[s], (((0,), (0,)), ((), ())), preferred_element_type=F32
            ).astype(BF16)


def legendre_sums(u, folded, legendre):
    owners, groups, _, both, fields = folded.shape
    _, _, _, latitudes, degrees = legendre.shape
    return pl.pallas_call(
        legendre_kernel,
        grid=(groups,),
        out_shape=jax.ShapeDtypeStruct((groups, 2, 2, fields, degrees), BF16),
        in_specs=[
            pl.BlockSpec((owners, None, 2, both, fields), lambda k: (0, k, 0, 0, 0)),
            pl.BlockSpec((None, None, 2, latitudes, degrees), lambda k: (k, u, 0, 0, 0)),
        ],
        out_specs=pl.BlockSpec((None, 2, 2, fields, degrees), lambda k: (k, 0, 0, 0, 0)),
        compiler_params=pltpu.CompilerParams(vmem_limit_bytes=48 * 2**20),
    )(folded, legendre)


def on_device(owners, grid_values, lon_counts, legendre):
    owned = legendre.shape[0]
    y, coarse, fine = prepare(grid_values, lon_counts, owners, owned)
    by_class = legendre.reshape(owned // 4, 4, *legendre.shape[1:])
    results = []
    for u in range(4):
        chunk = transform(u, y, coarse, fine)
        folded = lax.all_to_all(chunk, "lev", split_axis=0, concat_axis=0, tiled=True)
        partial_sums = legendre_sums(u, folded, by_class)
        results.append(lax.psum_scatter(partial_sums, "band", scatter_dimension=3, tiled=True))
    spectra = jnp.stack(results, axis=1)
    return spectra.reshape(owned, *spectra.shape[2:]).astype(F32)


def solution(mesh):
    return jax.shard_map(
        functools.partial(on_device, mesh.shape["lev"]),
        mesh=mesh,
        in_specs=(
            P(("band", "lev"), None, None, None),
            P(("band", "lev")),
            P("lev", None, "band", None),
        ),
        out_specs=P("lev", None, None, "band", None),
        check_vma=False,
    )
```

```python
import functools

import jax
import jax.numpy as jnp
from jax import lax
from jax.experimental import pallas as pl
from jax.experimental.pallas import tpu as pltpu
from jax.sharding import PartitionSpec as P

F32 = jnp.float32
BF16 = jnp.bfloat16
COS = (1.0, -19.73920440673828, 64.9390869140625, -85.4496078491211, 60.16310119628906, -25.950063705444336, 6.50340461730957)
SIN = (6.283182621002197, -41.341392517089844, 81.59541320800781, -76.57229614257812, 41.17121124267578, -12.217327117919922)
LANES = 128
ROWS = 4
MESH = pl.DeviceIdType.MESH


def poly(coefs, z):
    out = jnp.full_like(z, coefs[-1])
    for coef in coefs[-2::-1]:
        out = out * z + coef
    return out


def cos_sin(products, count, inverse):
    turns = jnp.floor(products * inverse + 0.5)
    t = (products - turns * count) * inverse
    z = t * t
    return poly(COS, z), t * poly(SIN, z)


def prepare_kernel(owners, owned, counts_ref, inverse_ref, x_ref, y_ref, coarse_ref, fine_ref):
    pair = pl.program_id(0)
    count = counts_ref[pair]
    quarter = lax.shift_right_logical(count, 2)
    fields, points = x_ref.shape[1:]
    width = points // 4
    tiles = width // LANES
    last = points - width - LANES
    rows = 16
    lane = lax.broadcasted_iota(jnp.int32, (rows, LANES), 1)
    starts, shifts = [], []
    for k in range(4):
        start = jnp.minimum(quarter * k // LANES * LANES, last)
        starts.append(start)
        shifts.append(quarter * k - start)

    def fold(step, carry):
        row = pl.ds(pl.multiple_of(step * rows, rows), rows)
        pieces = []
        for k in range(4):
            shift = shifts[k]
            both = []
            for h in range(2):
                turned = []
                for i in range(tiles + (k > 0)):
                    at = pl.multiple_of(starts[k] + i * LANES, LANES)
                    v = x_ref[h, row, pl.ds(at, LANES)].astype(F32)
                    if k:
                        v = pltpu.roll(v, (LANES - shift) & (LANES - 1), 1)
                    turned.append(v)
                if k:
                    keep = lane < LANES - shift
                    turned = [jnp.where(keep, turned[i], turned[i + 1]) for i in range(tiles)]
                both.append(turned)
            pieces.append([[n + s for n, s in zip(*both)], [n - s for n, s in zip(*both)]])
        for s in range(2):
            to = pl.ds(pl.multiple_of(step * rows + s * fields, rows), rows)
            for i in range(tiles):
                inside = lane + i * LANES < quarter
                x0, x1, x2, x3 = (jnp.where(inside, pieces[k][s][i], 0.0) for k in range(4))
                at = pl.ds(i * LANES, LANES)
                y_ref[0, to, at] = ((x0 + x2) + (x1 + x3)).astype(BF16)
                y_ref[1, to, at] = (x0 - x2).astype(BF16)
                y_ref[2, to, at] = ((x0 + x2) - (x1 + x3)).astype(BF16)
                y_ref[3, to, at] = (x1 - x3).astype(BF16)
        return carry

    lax.fori_loop(0, fields // rows, fold, 0)

    n = count.astype(F32)
    inverse = inverse_ref[pair]
    groups = owned // 4
    middle = 2 * groups - 2
    place = lax.broadcasted_iota(jnp.int32, (16, width), 1).astype(F32)
    row = lax.broadcasted_iota(jnp.int32, (16, width), 0).astype(F32)
    for step in range(groups // 2):
        c, s = cos_sin(place * float(4 * step + 2), n, inverse)
        fine_ref[step, 0] = c.astype(BF16)
        fine_ref[step, 1] = s.astype(BF16)
    owner_cos, owner_sin = cos_sin(place * (row * float(owned)), n, inverse)
    owner_cos, owner_sin = owner_cos * inverse, owner_sin * inverse
    for u in range(4):
        c, s = cos_sin(place * float(middle + u), n, inverse)
        coarse_ref[u, 0] = (owner_cos * c - owner_sin * s).astype(BF16)
        coarse_ref[u, 1] = (owner_sin * c + owner_cos * s).astype(BF16)


def prepare(grid_values, lon_counts, owners, owned):
    pairs, _, fields, points = grid_values.shape
    width = points // 4
    halves = owned // 8
    smem = pl.BlockSpec(memory_space=pltpu.SMEM)
    return pl.pallas_call(
        functools.partial(prepare_kernel, owners, owned),
        grid=(pairs,),
        out_shape=(
            jax.ShapeDtypeStruct((pairs, 4, 2 * fields, width), BF16),
            jax.ShapeDtypeStruct((pairs, 4, 2, owners, width), BF16),
            jax.ShapeDtypeStruct((pairs, halves, 2, owners, width), BF16),
        ),
        in_specs=[smem, smem, pl.BlockSpec((None, 2, fields, points), lambda p: (p, 0, 0, 0))],
        out_specs=(
            pl.BlockSpec((None, 4, 2 * fields, width), lambda p: (p, 0, 0, 0)),
            pl.BlockSpec((None, 4, 2, owners, width), lambda p: (p, 0, 0, 0, 0)),
            pl.BlockSpec((None, halves, 2, owners, width), lambda p: (p, 0, 0, 0, 0)),
        ),
        compiler_params=pltpu.CompilerParams(vmem_limit_bytes=48 * 2**20),
    )(lon_counts, 1.0 / lon_counts.astype(F32), grid_values)


def transform_kernel(a_ref, b_ref, coarse_ref, fine_ref, out_ref, table, total):
    u = pl.program_id(0)
    pair = pl.program_id(1)
    pairs = pl.num_programs(1)
    halves = fine_ref.shape[0]
    owners = coarse_ref.shape[1]
    fields = out_ref.shape[-1]
    for step in range(halves):
        for j, (k, l) in enumerate(((0, 0), (1, 0), (0, 1), (1, 1))):
            table[pl.ds((4 * step + j) * owners, owners), :] = coarse_ref[k] * fine_ref[step, l]
    spot = pl.ds(pair, owners, stride=8)

    def keep(t, real, imag):
        for r, value in enumerate((real, imag)):
            for s in range(2):
                total[4 * t + 2 * r + s, spot, :] = value[:, s * fields : (s + 1) * fields]

    def waves(ref):
        part = lax.dot_general(table[...], ref[...], (((1,), (1,)), ((), ())), preferred_element_type=F32)
        out = []
        for step in range(halves):
            cc, sc, cs, ss = (part[(4 * step + j) * owners : (4 * step + j + 1) * owners] for j in range(4))
            out.append((cc - ss, sc + cs, cc + ss, sc - cs))
        return out

    @pl.when(u % 2 == 0)
    def _():
        for step, (ca, sa, da, ta) in enumerate(waves(a_ref)):
            keep(halves + step, ca, -sa)
            keep(halves - 1 - step, da, -ta)

    @pl.when(u % 2 == 1)
    def _():
        sign = jnp.where(u == 1, 1.0, -1.0).astype(F32)
        for step, ((ca, sa, da, ta), (cb, sb, db, tb)) in enumerate(zip(waves(a_ref), waves(b_ref))):
            keep(halves + step, ca - sign * sb, -(sa + sign * cb))
            keep(halves - 1 - step, da - sign * tb, -(ta + sign * db))

    @pl.when(pair == pairs - 1)
    def _():
        for t in range(2 * halves):
            for s in range(2):
                real = total[4 * t + s].reshape(owners, 8, fields)
                imag = total[4 * t + 2 + s].reshape(owners, 8, fields)
                out_ref[:, t, s] = jnp.concatenate([real, imag], axis=1).astype(BF16)


def transform(y, coarse, fine):
    pairs, _, columns, width = y.shape
    halves, _, owners = fine.shape[1:4]
    fields = columns // 2
    return pl.pallas_call(
        transform_kernel,
        grid=(4, pairs),
        out_shape=jax.ShapeDtypeStruct((4, owners, 2 * halves, 2, 2 * pairs, fields), BF16),
        in_specs=[
            pl.BlockSpec((None, None, columns, width), lambda u, p: (p, u - u // 3 * 2, 0, 0)),
            pl.BlockSpec((None, None, columns, width), lambda u, p: (p * (u % 2), 3, 0, 0)),
            pl.BlockSpec((None, None, 2, owners, width), lambda u, p: (p, u, 0, 0, 0)),
            pl.BlockSpec((None, halves, 2, owners, width), lambda u, p: (p, 0, 0, 0, 0)),
        ],
        out_specs=pl.BlockSpec((None, owners, 2 * halves, 2, 2 * pairs, fields), lambda u, p: (u, 0, 0, 0, 0, 0)),
        scratch_shapes=[
            pltpu.VMEM((4 * halves * owners, width), BF16),
            pltpu.VMEM((8 * halves, owners * pairs, fields), F32),
        ],
        compiler_params=pltpu.CompilerParams(vmem_limit_bytes=48 * 2**20),
    )(y, y, coarse, fine)


def exchange_kernel(
    chunk, ahead, folded, legendre, out, inbox, weights, partial, from_core, first_out, from_first, second_out, from_second, staged,
    send_sem, recv_sem, weight_sem, core_send, core_recv, first_send, first_recv, second_send, second_recv, out_sem,
):
    _, owners, groups, _, both, fields = folded.shape
    degrees = legendre.shape[-1]
    pairs = both // 2
    per_class = groups // chunk
    chunks = 4 * per_class
    half = 2 * chunk
    block = fields // 8
    band, lev = lax.axis_index("band"), lax.axis_index("lev")
    chip, core = band // 2, band % 2
    beside = chip + 1 - 2 * (chip % 2)
    facing = 3 - chip
    opposite = (chip + 2) % 4
    first, second = (beside, facing), (facing, beside)
    sibling = {"band": chip * 2 + 1 - core}

    def on_chip(c):
        return {"band": c * 2 + core}

    def owner(d):
        return {"lev": d}

    def place(c):
        return c // per_class, pl.ds(c % per_class * chunk, chunk)

    barrier = pltpu.get_barrier_semaphore()
    for j in range(1, owners):
        pl.semaphore_signal(barrier, inc=1, device_id=owner((lev + j) % owners), device_id_type=MESH)
    for device in (sibling, on_chip(beside), on_chip(facing)):
        pl.semaphore_signal(barrier, inc=1, device_id=device, device_id_type=MESH)
    pl.semaphore_wait(barrier, owners + 2)

    def to_owner(c, d):
        u, t = place(c)
        return pltpu.make_async_remote_copy(
            src_ref=folded.at[u, d, t],
            dst_ref=inbox.at[c, lev],
            send_sem=send_sem.at[c, d],
            recv_sem=recv_sem.at[c, lev],
            device_id=owner(d),
            device_id_type=MESH,
        )

    def from_owner(c, d):
        u, t = place(c)
        return pltpu.make_async_remote_copy(
            src_ref=folded.at[u, d, t],
            dst_ref=inbox.at[c, d],
            send_sem=send_sem.at[c, d],
            recv_sem=recv_sem.at[c, d],
            device_id=owner(d),
            device_id_type=MESH,
        )

    def own(c):
        u, t = place(c)
        return pltpu.make_async_copy(folded.at[u, lev, t], inbox.at[c, lev], recv_sem.at[c, lev])

    def weight(c):
        u, t = place(c)
        return pltpu.make_async_copy(legendre.at[t, u], weights.at[c], weight_sem.at[c])

    def across(c):
        return pltpu.make_async_remote_copy(
            src_ref=partial.at[c % 4, 1 - core],
            dst_ref=from_core.at[c],
            send_sem=core_send.at[c],
            recv_sem=core_recv.at[c],
            device_id=sibling,
            device_id_type=MESH,
        )

    def first_step(c, v):
        return pltpu.make_async_remote_copy(
            src_ref=first_out.at[c % 2, v],
            dst_ref=from_first.at[c, v],
            send_sem=first_send.at[c, v],
            recv_sem=first_recv.at[c, v],
            device_id=on_chip(first[v]),
            device_id_type=MESH,
        )

    def second_step(c, v):
        return pltpu.make_async_remote_copy(
            src_ref=second_out.at[c % 2, v],
            dst_ref=from_second.at[c, v],
            send_sem=second_send.at[c, v],
            recv_sem=second_recv.at[c, v],
            device_id=on_chip(second[v]),
            device_id_type=MESH,
        )

    def result(c):
        u, t = place(c)
        return pltpu.make_async_copy(staged.at[c % 2], out.at[t, u], out_sem.at[c])

    def launch(c):
        own(c).start()
        weight(c).start()

        def one(j, carry):
            to_owner(c, (lev + j) % owners).start()
            return carry

        lax.fori_loop(1, owners, one, 0)

    def sums(c):
        own(c).wait()
        weight(c).wait()

        def one(j, carry):
            from_owner(c, (lev + j) % owners).wait_recv()
            to_owner(c, (lev + j) % owners).wait_send()
            return carry

        lax.fori_loop(1, owners, one, 0)

        def wave(t, carry):
            for s in range(2):
                f = inbox[c, :, t, s].astype(F32).reshape(owners, 2, pairs, fields)
                part = jnp.concatenate(
                    [f[:, r].reshape(owners * pairs, fields) for r in range(2)], axis=1
                ).astype(BF16)
                total = lax.dot_general(
                    part, weights[c, t, s], (((0,), (0,)), ((), ())), preferred_element_type=F32
                ).astype(BF16)
                for r in range(2):
                    for b in range(8):
                        at = r * fields + b * block
                        partial[c % 4, b % 2, b // 2, 4 * t + 2 * s + r] = total[at : at + block]
            return carry

        lax.fori_loop(0, chunk, wave, 0)
        across(c).start()

    def parts(c, v, row, target):
        at = pl.ds(v * half + row, ROWS)
        return partial[c % 4, core, target, at].astype(F32) + from_core[c, target, at].astype(F32)

    def rows(body):
        def one(i, carry):
            body(i * ROWS)
            return carry

        lax.fori_loop(0, half // ROWS, one, 0)

    def first_stage(c):
        across(c).wait()
        for v in range(2):

            def add(row):
                for w, target in enumerate((first[v], opposite)):
                    first_out[c % 2, v, w, pl.ds(row, ROWS)] = parts(c, v, row, target).astype(BF16)

            rows(add)
            first_step(c, v).start()

    def second_stage(c):
        for v in range(2):
            first_step(c, v).wait()

            def add(row):
                at = pl.ds(row, ROWS)
                both = parts(c, v, row, second[v]) + from_first[c, v, 1, at].astype(F32)
                second_out[c % 2, v, at] = both.astype(BF16)

            rows(add)
            second_step(c, v).start()

    def last_stage(c):
        @pl.when(c >= 2)
        def _():
            result(c - 2).wait()

        for v in range(2):
            second_step(c, v).wait()

            def add(row):
                at = pl.ds(row, ROWS)
                both = parts(c, v, row, chip) + from_first[c, v, 0, at].astype(F32) + from_second[c, v, at].astype(F32)
                for i in range(ROWS // 4):
                    staged[c % 2, v * (chunk // 2) + row // 4 + i] = both[4 * i : 4 * i + 4].astype(BF16)

            rows(add)
        result(c).start()

    for c in range(ahead):
        launch(c)

    def turn(c, carry):
        @pl.when(c + ahead < chunks)
        def _():
            launch(c + ahead)

        @pl.when(c < chunks)
        def _():
            sums(c)

        @pl.when((c >= 1) & (c <= chunks))
        def _():
            first_stage(c - 1)

        @pl.when((c >= 2) & (c <= chunks + 1))
        def _():
            second_stage(c - 2)

        @pl.when(c >= 3)
        def _():
            last_stage(c - 3)

        return carry

    lax.fori_loop(0, chunks + 3, turn, 0)
    result(chunks - 2).wait()
    result(chunks - 1).wait()


def exchange(folded, legendre, chunk, ahead):
    _, owners, groups, _, both, fields = folded.shape
    _, _, _, latitudes, degrees = legendre.shape
    chunks = 4 * groups // chunk
    half = 2 * chunk
    block = fields // 8
    dma = pltpu.SemaphoreType.DMA
    anywhere = pl.BlockSpec(memory_space=pl.ANY)
    return pl.pallas_call(
        functools.partial(exchange_kernel, chunk, ahead),
        out_shape=jax.ShapeDtypeStruct((groups, 4, 4, block, degrees), BF16),
        in_specs=[anywhere, anywhere],
        out_specs=anywhere,
        scratch_shapes=[
            pltpu.VMEM((chunks, owners, chunk, 2, both, fields), BF16),
            pltpu.VMEM((chunks, chunk, 2, latitudes, degrees), BF16),
            pltpu.VMEM((4, 2, 4, 2 * half, block, degrees), BF16),
            pltpu.VMEM((chunks, 4, 2 * half, block, degrees), BF16),
            pltpu.VMEM((2, 2, 2, half, block, degrees), BF16),
            pltpu.VMEM((chunks, 2, 2, half, block, degrees), BF16),
            pltpu.VMEM((2, 2, half, block, degrees), BF16),
            pltpu.VMEM((chunks, 2, half, block, degrees), BF16),
            pltpu.VMEM((2, chunk, 4, block, degrees), BF16),
            dma((chunks, owners)),
            dma((chunks, owners)),
            dma((chunks,)),
            dma((chunks,)),
            dma((chunks,)),
            dma((chunks, 2)),
            dma((chunks, 2)),
            dma((chunks, 2)),
            dma((chunks, 2)),
            dma((chunks,)),
        ],
        compiler_params=pltpu.CompilerParams(
            collective_id=0, has_side_effects=True, vmem_limit_bytes=60 * 2**20
        ),
    )(folded, legendre)


CHUNK = 6
AHEAD = 2


def on_device(owners, grid_values, lon_counts, legendre):
    owned = legendre.shape[0]
    y, coarse, fine = prepare(grid_values, lon_counts, owners, owned)
    folded = transform(y, coarse, fine)
    by_class = legendre.reshape(owned // 4, 4, *legendre.shape[1:])
    spectra = exchange(folded, by_class, CHUNK, AHEAD)
    return spectra.reshape(owned, 2, 2, *spectra.shape[3:]).astype(F32)


def solution(mesh):
    return jax.shard_map(
        functools.partial(on_device, mesh.shape["lev"]),
        mesh=mesh,
        in_specs=(
            P(("band", "lev"), None, None, None),
            P(("band", "lev")),
            P("lev", None, "band", None),
        ),
        out_specs=P("lev", None, None, "band", None),
        check_vma=False,
    )
```

```python
import functools

import jax
import jax.numpy as jnp
from jax import lax
from jax.experimental import pallas as pl
from jax.experimental.pallas import tpu as pltpu
from jax.sharding import PartitionSpec as P

F32 = jnp.float32
BF16 = jnp.bfloat16
COS = (1.0, -19.73920440673828, 64.9390869140625, -85.4496078491211, 60.16310119628906, -25.950063705444336, 6.50340461730957)
SIN = (6.283182621002197, -41.341392517089844, 81.59541320800781, -76.57229614257812, 41.17121124267578, -12.217327117919922)
LANES = 128
ROWS = 4
MESH = pl.DeviceIdType.MESH


def poly(coefs, z):
    out = jnp.full_like(z, coefs[-1])
    for coef in coefs[-2::-1]:
        out = out * z + coef
    return out


def cos_sin(products, count, inverse):
    turns = jnp.floor(products * inverse + 0.5)
    t = (products - turns * count) * inverse
    z = t * t
    return poly(COS, z), t * poly(SIN, z)


def prepare_kernel(owners, owned, counts_ref, inverse_ref, x_ref, y_ref, coarse_ref, fine_ref):
    pair = pl.program_id(0)
    count = counts_ref[pair]
    quarter = lax.shift_right_logical(count, 2)
    fields, points = x_ref.shape[1:]
    width = points // 4
    tiles = width // LANES
    last = points - width - LANES
    rows = 16
    lane = lax.broadcasted_iota(jnp.int32, (rows, LANES), 1)
    starts, shifts = [], []
    for k in range(4):
        start = jnp.minimum(quarter * k // LANES * LANES, last)
        starts.append(start)
        shifts.append(quarter * k - start)

    def fold(step, carry):
        row = pl.ds(pl.multiple_of(step * rows, rows), rows)
        pieces = []
        for k in range(4):
            shift = shifts[k]
            both = []
            for h in range(2):
                turned = []
                for i in range(tiles + (k > 0)):
                    at = pl.multiple_of(starts[k] + i * LANES, LANES)
                    v = x_ref[h, row, pl.ds(at, LANES)].astype(F32)
                    if k:
                        v = pltpu.roll(v, (LANES - shift) & (LANES - 1), 1)
                    turned.append(v)
                if k:
                    keep = lane < LANES - shift
                    turned = [jnp.where(keep, turned[i], turned[i + 1]) for i in range(tiles)]
                both.append(turned)
            pieces.append([[n + s for n, s in zip(*both)], [n - s for n, s in zip(*both)]])
        for s in range(2):
            to = pl.ds(pl.multiple_of(step * rows + s * fields, rows), rows)
            for i in range(tiles):
                inside = lane + i * LANES < quarter
                x0, x1, x2, x3 = (pieces[k][s][i] for k in range(4))
                if (i + 1) * LANES > points // 8:
                    x0, x1, x2, x3 = (jnp.where(inside, x, 0.0) for x in (x0, x1, x2, x3))
                at = pl.ds(i * LANES, LANES)
                y_ref[0, to, at] = ((x0 + x2) + (x1 + x3)).astype(BF16)
                y_ref[1, to, at] = (x0 - x2).astype(BF16)
                y_ref[2, to, at] = ((x0 + x2) - (x1 + x3)).astype(BF16)
                y_ref[3, to, at] = (x1 - x3).astype(BF16)
        return carry

    lax.fori_loop(0, fields // rows, fold, 0)

    n = count.astype(F32)
    inverse = inverse_ref[pair]
    groups = owned // 4
    middle = 2 * groups - 2
    place = lax.broadcasted_iota(jnp.int32, (16, width), 1).astype(F32)
    row = lax.broadcasted_iota(jnp.int32, (16, width), 0).astype(F32)
    rates = jnp.where(row < 8, 4 * row + 2, row + float(middle - 8))
    near_cos, near_sin = cos_sin(place * rates, n, inverse)
    for step in range(groups // 2):
        for r, near in enumerate((near_cos, near_sin)):
            fine_ref[step, r] = jnp.broadcast_to(near[step : step + 1], (16, width)).astype(BF16)
    owner_cos, owner_sin = cos_sin(place * (row * float(owned)), n, inverse)
    owner_cos, owner_sin = owner_cos * inverse, owner_sin * inverse
    for u in range(4):
        c, s = near_cos[8 + u : 9 + u], near_sin[8 + u : 9 + u]
        coarse_ref[u, 0] = (owner_cos * c - owner_sin * s).astype(BF16)
        coarse_ref[u, 1] = (owner_sin * c + owner_cos * s).astype(BF16)


def prepare(grid_values, lon_counts, owners, owned):
    pairs, _, fields, points = grid_values.shape
    width = points // 4
    halves = owned // 8
    smem = pl.BlockSpec(memory_space=pltpu.SMEM)
    return pl.pallas_call(
        functools.partial(prepare_kernel, owners, owned),
        grid=(pairs,),
        out_shape=(
            jax.ShapeDtypeStruct((pairs, 4, 2 * fields, width), BF16),
            jax.ShapeDtypeStruct((pairs, 4, 2, owners, width), BF16),
            jax.ShapeDtypeStruct((pairs, halves, 2, owners, width), BF16),
        ),
        in_specs=[smem, smem, pl.BlockSpec((None, 2, fields, points), lambda p: (p, 0, 0, 0))],
        out_specs=(
            pl.BlockSpec((None, 4, 2 * fields, width), lambda p: (p, 0, 0, 0)),
            pl.BlockSpec((None, 4, 2, owners, width), lambda p: (p, 0, 0, 0, 0)),
            pl.BlockSpec((None, halves, 2, owners, width), lambda p: (p, 0, 0, 0, 0)),
        ),
        compiler_params=pltpu.CompilerParams(vmem_limit_bytes=48 * 2**20),
    )(lon_counts, 1.0 / lon_counts.astype(F32), grid_values)


def exchange_kernel(
    chunk, ahead, coarse, fine, y, legendre, out,
    samples, table, total, folded, inbox, weights, partial, from_core, first_out, from_first, second_out, from_second, staged,
    sample_sem, send_sem, recv_sem, weight_sem, core_send, core_recv, first_send, first_recv, second_send, second_recv, out_sem,
):
    _, owners, groups, _, both, fields = folded.shape
    degrees = legendre.shape[-1]
    pairs = both // 2
    per_class = groups // chunk
    chunks = 4 * per_class
    half = 2 * chunk
    block = fields // 8
    band, lev = lax.axis_index("band"), lax.axis_index("lev")
    chip, core = band // 2, band % 2
    beside = chip + 1 - 2 * (chip % 2)
    facing = 3 - chip
    opposite = (chip + 2) % 4
    first, second = (beside, facing), (facing, beside)
    sibling = {"band": chip * 2 + 1 - core}

    def on_chip(c):
        return {"band": c * 2 + core}

    def owner(d):
        return {"lev": d}

    def place(c):
        return c // per_class, pl.ds(c % per_class * chunk, chunk)

    count = y.shape[0]
    halves = groups // 2

    def sample(g, part):
        u, p = g // count, g % count
        kind = 3 if part else u - u // 3 * 2
        return pltpu.make_async_copy(y.at[p, kind], samples.at[g % 2, part], sample_sem.at[g % 2, part])

    def fetch(g):
        sample(g, 0).start()

        @pl.when(g // count % 2 == 1)
        def _():
            sample(g, 1).start()

    def transform(g):
        u, p = g // count, g % count

        @pl.when(g + 1 < 4 * count)
        def _():
            fetch(g + 1)

        for step in range(halves):
            for j, (k, l) in enumerate(((0, 0), (1, 0), (0, 1), (1, 1))):
                table[pl.ds((4 * step + j) * owners, owners), :] = coarse[p, u, k] * fine[p, step, l]
        spot = pl.ds(p, owners, stride=8)

        def keep(t, real, imag):
            for r, value in enumerate((real, imag)):
                for s in range(2):
                    total[4 * t + 2 * r + s, spot, :] = value[:, s * fields : (s + 1) * fields]

        def waves(part):
            sums = lax.dot_general(
                table[...], samples[g % 2, part], (((1,), (1,)), ((), ())), preferred_element_type=F32
            )
            found = []
            for step in range(halves):
                cc, sc, cs, ss = (sums[(4 * step + j) * owners : (4 * step + j + 1) * owners] for j in range(4))
                found.append((cc - ss, sc + cs, cc + ss, sc - cs))
            return found

        sample(g, 0).wait()

        @pl.when(u % 2 == 0)
        def _():
            for step, (ca, sa, da, ta) in enumerate(waves(0)):
                keep(halves + step, ca, -sa)
                keep(halves - 1 - step, da, -ta)

        @pl.when(u % 2 == 1)
        def _():
            sample(g, 1).wait()
            sign = (2 - u).astype(F32)
            for step, ((ca, sa, da, ta), (cb, sb, db, tb)) in enumerate(zip(waves(0), waves(1))):
                keep(halves + step, ca - sign * sb, -(sa + sign * cb))
                keep(halves - 1 - step, da - sign * tb, -(ta + sign * db))

        @pl.when(p == count - 1)
        def _():
            def pack(t, carry):
                for s in range(2):
                    real = total[4 * t + s].reshape(owners, pairs, fields)
                    imag = total[4 * t + 2 + s].reshape(owners, pairs, fields)
                    folded[u, :, t, s] = jnp.concatenate([real, imag], axis=1).astype(BF16)
                return carry

            lax.fori_loop(0, groups, pack, 0)

    def transform_part(q):
        u, i = q // per_class, q % per_class

        def one(p, carry):
            transform(u * count + p)
            return carry

        lax.fori_loop(i * count // per_class, (i + 1) * count // per_class, one, 0)

    fetch(0)
    barrier = pltpu.get_barrier_semaphore()
    for j in range(1, owners):
        pl.semaphore_signal(barrier, inc=1, device_id=owner((lev + j) % owners), device_id_type=MESH)
    for device in (sibling, on_chip(beside), on_chip(facing)):
        pl.semaphore_signal(barrier, inc=1, device_id=device, device_id_type=MESH)
    pl.semaphore_wait(barrier, owners + 2)

    def to_owner(c, d):
        u, t = place(c)
        return pltpu.make_async_remote_copy(
            src_ref=folded.at[u, d, t],
            dst_ref=inbox.at[c, lev],
            send_sem=send_sem.at[c, d],
            recv_sem=recv_sem.at[c, lev],
            device_id=owner(d),
            device_id_type=MESH,
        )

    def from_owner(c, d):
        u, t = place(c)
        return pltpu.make_async_remote_copy(
            src_ref=folded.at[u, d, t],
            dst_ref=inbox.at[c, d],
            send_sem=send_sem.at[c, d],
            recv_sem=recv_sem.at[c, d],
            device_id=owner(d),
            device_id_type=MESH,
        )

    def own(c):
        u, t = place(c)
        return pltpu.make_async_copy(folded.at[u, lev, t], inbox.at[c, lev], recv_sem.at[c, lev])

    def weight(c):
        u, t = place(c)
        return pltpu.make_async_copy(legendre.at[t, u], weights.at[c % (ahead + 1)], weight_sem.at[c])

    def across(c):
        return pltpu.make_async_remote_copy(
            src_ref=partial.at[c % 4, 1 - core],
            dst_ref=from_core.at[c],
            send_sem=core_send.at[c],
            recv_sem=core_recv.at[c],
            device_id=sibling,
            device_id_type=MESH,
        )

    def first_step(c, v):
        return pltpu.make_async_remote_copy(
            src_ref=first_out.at[c % 2, v],
            dst_ref=from_first.at[c, v],
            send_sem=first_send.at[c, v],
            recv_sem=first_recv.at[c, v],
            device_id=on_chip(first[v]),
            device_id_type=MESH,
        )

    def second_step(c, v):
        return pltpu.make_async_remote_copy(
            src_ref=second_out.at[c % 2, v],
            dst_ref=from_second.at[c, v],
            send_sem=second_send.at[c, v],
            recv_sem=second_recv.at[c, v],
            device_id=on_chip(second[v]),
            device_id_type=MESH,
        )

    def result(c):
        u, t = place(c)
        return pltpu.make_async_copy(staged.at[c % 2], out.at[t, u], out_sem.at[c])

    def launch(c):
        own(c).start()
        weight(c).start()

        def one(j, carry):
            to_owner(c, (lev + j) % owners).start()
            return carry

        lax.fori_loop(1, owners, one, 0)

    def sums(c):
        own(c).wait()
        weight(c).wait()

        def one(j, carry):
            from_owner(c, (lev + j) % owners).wait_recv()
            to_owner(c, (lev + j) % owners).wait_send()
            return carry

        lax.fori_loop(1, owners, one, 0)

        def wave(t, carry):
            for s in range(2):
                f = inbox[c, :, t, s].astype(F32).reshape(owners, 2, pairs, fields)
                part = jnp.concatenate(
                    [f[:, r].reshape(owners * pairs, fields) for r in range(2)], axis=1
                ).astype(BF16)
                total = lax.dot_general(
                    part, weights[c % (ahead + 1), t, s], (((0,), (0,)), ((), ())), preferred_element_type=F32
                ).astype(BF16)
                for r in range(2):
                    for b in range(8):
                        at = r * fields + b * block
                        partial[c % 4, b % 2, b // 2, 4 * t + 2 * s + r] = total[at : at + block]
            return carry

        lax.fori_loop(0, chunk, wave, 0)
        across(c).start()

    def parts(c, v, row, target):
        at = pl.ds(v * half + row, ROWS)
        return partial[c % 4, core, target, at].astype(F32) + from_core[c, target, at].astype(F32)

    def rows(body):
        def one(i, carry):
            body(i * ROWS)
            return carry

        lax.fori_loop(0, half // ROWS, one, 0)

    def first_stage(c):
        across(c).wait()
        for v in range(2):

            def add(row):
                for w, target in enumerate((first[v], opposite)):
                    first_out[c % 2, v, w, pl.ds(row, ROWS)] = parts(c, v, row, target).astype(BF16)

            rows(add)
            first_step(c, v).start()

    def second_stage(c):
        for v in range(2):
            first_step(c, v).wait()

            def add(row):
                at = pl.ds(row, ROWS)
                both = parts(c, v, row, second[v]) + from_first[c, v, 1, at].astype(F32)
                second_out[c % 2, v, at] = both.astype(BF16)

            rows(add)
            second_step(c, v).start()

    def last_stage(c):
        @pl.when(c >= 2)
        def _():
            result(c - 2).wait()

        for v in range(2):
            second_step(c, v).wait()

            def add(row):
                at = pl.ds(row, ROWS)
                both = parts(c, v, row, chip) + from_first[c, v, 0, at].astype(F32) + from_second[c, v, at].astype(F32)
                for i in range(ROWS // 4):
                    staged[c % 2, v * (chunk // 2) + row // 4 + i] = both[4 * i : 4 * i + 4].astype(BF16)

            rows(add)
        result(c).start()

    for q in range(per_class):
        transform_part(q)
    for c in range(ahead):
        launch(c)
    for q in range(per_class, per_class + ahead - 1):
        transform_part(q)

    def turn(c, carry):
        @pl.when(c + ahead + per_class - 1 < chunks)
        def _():
            transform_part(c + ahead + per_class - 1)

        @pl.when(c + ahead < chunks)
        def _():
            launch(c + ahead)

        @pl.when(c < chunks)
        def _():
            sums(c)

        @pl.when((c >= 1) & (c <= chunks))
        def _():
            first_stage(c - 1)

        @pl.when((c >= 2) & (c <= chunks + 1))
        def _():
            second_stage(c - 2)

        @pl.when(c >= 3)
        def _():
            last_stage(c - 3)

        return carry

    lax.fori_loop(0, chunks + 3, turn, 0)
    result(chunks - 2).wait()
    result(chunks - 1).wait()


def exchange(y, coarse, fine, legendre, chunk, ahead):
    count, _, columns, width = y.shape
    owners, fields, both = coarse.shape[3], columns // 2, 2 * count
    groups, _, _, latitudes, degrees = legendre.shape
    chunks = 4 * groups // chunk
    half = 2 * chunk
    block = fields // 8
    dma = pltpu.SemaphoreType.DMA
    anywhere = pl.BlockSpec(memory_space=pl.ANY)
    inside = pl.BlockSpec(memory_space=pltpu.VMEM)
    return pl.pallas_call(
        functools.partial(exchange_kernel, chunk, ahead),
        out_shape=jax.ShapeDtypeStruct((groups, 4, 4, block, degrees), BF16),
        in_specs=[inside, inside, anywhere, anywhere],
        out_specs=anywhere,
        scratch_shapes=[
            pltpu.VMEM((2, 2, columns, width), BF16),
            pltpu.VMEM((2 * groups * owners, width), BF16),
            pltpu.VMEM((4 * groups, owners * count, fields), F32),
            pltpu.VMEM((4, owners, groups, 2, both, fields), BF16),
            pltpu.VMEM((chunks, owners, chunk, 2, both, fields), BF16),
            pltpu.VMEM((ahead + 1, chunk, 2, latitudes, degrees), BF16),
            pltpu.VMEM((4, 2, 4, 2 * half, block, degrees), BF16),
            pltpu.VMEM((chunks, 4, 2 * half, block, degrees), BF16),
            pltpu.VMEM((2, 2, 2, half, block, degrees), BF16),
            pltpu.VMEM((chunks, 2, 2, half, block, degrees), BF16),
            pltpu.VMEM((2, 2, half, block, degrees), BF16),
            pltpu.VMEM((chunks, 2, half, block, degrees), BF16),
            pltpu.VMEM((2, chunk, 4, block, degrees), BF16),
            dma((2, 2)),
            dma((chunks, owners)),
            dma((chunks, owners)),
            dma((chunks,)),
            dma((chunks,)),
            dma((chunks,)),
            dma((chunks, 2)),
            dma((chunks, 2)),
            dma((chunks, 2)),
            dma((chunks, 2)),
            dma((chunks,)),
        ],
        compiler_params=pltpu.CompilerParams(
            collective_id=0, has_side_effects=True, vmem_limit_bytes=60 * 2**20
        ),
    )(coarse, fine, y, legendre)


CHUNK = 4
AHEAD = 2


def on_device(owners, grid_values, lon_counts, legendre):
    owned = legendre.shape[0]
    y, coarse, fine = prepare(grid_values, lon_counts, owners, owned)
    by_class = legendre.reshape(owned // 4, 4, *legendre.shape[1:])
    spectra = exchange(y, coarse, fine, by_class, CHUNK, AHEAD)
    return spectra.reshape(owned, 2, 2, *spectra.shape[3:]).astype(F32)


def solution(mesh):
    return jax.shard_map(
        functools.partial(on_device, mesh.shape["lev"]),
        mesh=mesh,
        in_specs=(
            P(("band", "lev"), None, None, None),
            P(("band", "lev")),
            P("lev", None, "band", None),
        ),
        out_specs=P("lev", None, None, "band", None),
        check_vma=False,
    )
```

```python
import functools

import jax
import jax.numpy as jnp
from jax import lax
from jax.experimental import pallas as pl
from jax.experimental.pallas import tpu as pltpu
from jax.sharding import PartitionSpec as P

F32 = jnp.float32
BF16 = jnp.bfloat16
COS = (1.0, -19.73920440673828, 64.9390869140625, -85.4496078491211, 60.16310119628906, -25.950063705444336, 6.50340461730957)
SIN = (6.283182621002197, -41.341392517089844, 81.59541320800781, -76.57229614257812, 41.17121124267578, -12.217327117919922)
LANES = 128
ROWS = 4
MESH = pl.DeviceIdType.MESH


def poly(coefs, z):
    out = jnp.full_like(z, coefs[-1])
    for coef in coefs[-2::-1]:
        out = out * z + coef
    return out


def cos_sin(products, count, inverse):
    turns = jnp.floor(products * inverse + 0.5)
    t = (products - turns * count) * inverse
    z = t * t
    return poly(COS, z), t * poly(SIN, z)


def fill_table(table, halves, owners, coarse, fine):
    for step in range(halves):
        for j, (k, l) in enumerate(((0, 0), (1, 0), (0, 1), (1, 1))):
            table[pl.ds((4 * step + j) * owners, owners), :] = coarse(k) * fine(step, l)


def transform_waves(table, rows, parts, halves, owners):
    sums = lax.dot_general(table[...], rows, (((1,), (1,)), ((), ())), preferred_element_type=F32)
    width = rows.shape[0] // parts
    found = []
    for step in range(halves):
        for part in range(parts):
            at = slice(part * width, (part + 1) * width)
            cc, sc, cs, ss = (sums[(4 * step + j) * owners : (4 * step + j + 1) * owners, at] for j in range(4))
            found.append((cc - ss, sc + cs, cc + ss, sc - cs))
    return found


def keep_wave(total, spot, fields, t, real, imag):
    for r, value in enumerate((real, imag)):
        for s in range(2):
            total[4 * t + 2 * r + s, spot, :] = value[:, s * fields : (s + 1) * fields]


def pack_waves(total, groups, owners, pairs, fields, store):
    def pack(t, carry):
        for s in range(2):
            real = total[4 * t + s].reshape(owners, pairs, fields)
            imag = total[4 * t + 2 + s].reshape(owners, pairs, fields)
            store(t, s, jnp.concatenate([real, imag], axis=1).astype(BF16))
        return carry

    lax.fori_loop(0, groups, pack, 0)


def prepare_kernel(owners, owned, counts_ref, x_ref, y_ref, coarse_ref, fine_ref, folded_ref, sum_ref, table, total):
    pair = pl.program_id(0)
    count = counts_ref[pair]
    quarter = lax.shift_right_logical(count, 2)
    fields, points = x_ref.shape[1:]
    width = points // 4
    tiles = width // LANES
    last = points - width - LANES
    rows = 16
    lane = lax.broadcasted_iota(jnp.int32, (rows, LANES), 1)
    starts, shifts = [], []
    for k in range(4):
        start = jnp.minimum(quarter * k // LANES * LANES, last)
        starts.append(start)
        shifts.append(quarter * k - start)

    def fold(step, carry):
        row = pl.ds(pl.multiple_of(step * rows, rows), rows)
        keeps = [lane < LANES - shifts[k] for k in range(4)]

        def turned(k, h, i):
            v = x_ref[h, row, pl.ds(pl.multiple_of(starts[k] + i * LANES, LANES), LANES)]
            return pltpu.roll(v, (LANES - shifts[k]) & (LANES - 1), 1) if k else v

        before = {(k, h): turned(k, h, 0) for k in range(1, 4) for h in range(2)}
        for i in range(tiles):
            at = pl.ds(i * LANES, LANES)
            quarters = []
            for k in range(4):
                both = []
                for h in range(2):
                    if k:
                        after = turned(k, h, i + 1)
                        v = jnp.where(keeps[k], before[k, h], after)
                        before[k, h] = after
                    else:
                        v = turned(k, h, i)
                    both.append(v.astype(F32))
                quarters.append((both[0] + both[1], both[0] - both[1]))
            inside = lane + i * LANES < quarter
            for s in range(2):
                to = pl.ds(pl.multiple_of(step * rows + s * fields, rows), rows)
                x0, x1, x2, x3 = (quarters[k][s] for k in range(4))
                even, odd = x0 + x2, x1 + x3
                for kind, v in enumerate((even + odd, x0 - x2, even - odd, x1 - x3)):
                    if (i + 1) * LANES > points // 8:
                        v = jnp.where(inside, v, 0.0)
                    if kind:
                        y_ref[kind - 1, to, at] = v.astype(BF16)
                    else:
                        sum_ref[to, at] = v.astype(BF16)
        return carry

    lax.fori_loop(0, fields // rows, fold, 0, unroll=2)

    n = count.astype(F32)
    inverse = 1.0 / jnp.full((16, width), n, F32)
    groups = owned // 4
    middle = 2 * groups - 2
    place = lax.broadcasted_iota(jnp.int32, (16, width), 1).astype(F32)
    row = lax.broadcasted_iota(jnp.int32, (16, width), 0).astype(F32)
    rates = jnp.where(row < 8, 4 * row + 2, row + float(middle - 8))
    near_cos, near_sin = cos_sin(place * rates, n, inverse)
    fine_ref[0] = near_cos[:8]
    fine_ref[1] = near_sin[:8]
    owner_cos, owner_sin = cos_sin(place * (row * float(owned)), n, inverse)
    owner_cos, owner_sin = owner_cos * inverse, owner_sin * inverse
    for u in range(4):
        c, s = near_cos[8 + u : 9 + u], near_sin[8 + u : 9 + u]
        far = (owner_cos * c - owner_sin * s).astype(BF16), (owner_sin * c + owner_cos * s).astype(BF16)
        if u:
            coarse_ref[u - 1, 0], coarse_ref[u - 1, 1] = far
        else:
            halves = groups // 2
            near = near_cos, near_sin

            def fine(step, l):
                return jnp.broadcast_to(near[l][step : step + 1], (16, width)).astype(BF16)

            fill_table(table, halves, owners, lambda k: far[k], fine)
            spot = pl.ds(pair, owners, stride=8)
            waves = transform_waves(table, sum_ref[...], 1, halves, owners)
            for step, (ca, sa, da, ta) in enumerate(waves):
                keep_wave(total, spot, fields, halves + step, ca, -sa)
                keep_wave(total, spot, fields, halves - 1 - step, da, -ta)

    @pl.when(pair == pl.num_programs(0) - 1)
    def _():
        def store(t, s, value):
            folded_ref[:, t, s] = value

        pack_waves(total, groups, owners, 8, fields, store)


def prepare(grid_values, lon_counts, owners, owned):
    pairs, _, fields, points = grid_values.shape
    width = points // 4
    groups = owned // 4
    smem = pl.BlockSpec(memory_space=pltpu.SMEM)
    folded = (owners, groups, 2, 2 * pairs, fields)
    return pl.pallas_call(
        functools.partial(prepare_kernel, owners, owned),
        grid=(pairs,),
        out_shape=(
            jax.ShapeDtypeStruct((pairs, 3, 2 * fields, width), BF16),
            jax.ShapeDtypeStruct((pairs, 3, 2, owners, width), BF16),
            jax.ShapeDtypeStruct((pairs, 2, 8, width), F32),
            jax.ShapeDtypeStruct(folded, BF16),
        ),
        in_specs=[smem, pl.BlockSpec((None, 2, fields, points), lambda p: (p, 0, 0, 0))],
        out_specs=(
            pl.BlockSpec((None, 3, 2 * fields, width), lambda p: (p, 0, 0, 0)),
            pl.BlockSpec((None, 3, 2, owners, width), lambda p: (p, 0, 0, 0, 0)),
            pl.BlockSpec((None, 2, 8, width), lambda p: (p, 0, 0, 0)),
            pl.BlockSpec(folded, lambda p: (0, 0, 0, 0, 0)),
        ),
        scratch_shapes=[
            pltpu.VMEM((2 * fields, width), BF16),
            pltpu.VMEM((2 * groups * owners, width), BF16),
            pltpu.VMEM((4 * groups, owners * pairs, fields), F32),
        ],
        compiler_params=pltpu.CompilerParams(vmem_limit_bytes=60 * 2**20),
    )(lon_counts, grid_values)


def exchange_kernel(
    chunk, ahead, gap, far_hbm, near_hbm, first_class, y, legendre, out,
    near, far, samples, table, total, folded, inbox, weights, partial, from_core, first_out, from_first, second_out, from_second, staged,
    factor_sem, sample_sem, send_sem, recv_sem, weight_sem, core_send, core_recv, first_send, first_recv, second_send, second_recv, out_sem,
):
    _, owners, groups, _, both, fields = folded.shape
    degrees = legendre.shape[-1]
    pairs = both // 2
    per_class = groups // chunk
    chunks = 4 * per_class
    half = 2 * chunk
    block = fields // 8
    band, lev = lax.axis_index("band"), lax.axis_index("lev")
    chip, core = band // 2, band % 2
    beside = chip + 1 - 2 * (chip % 2)
    facing = 3 - chip
    opposite = (chip + 2) % 4
    first, second = (beside, facing), (facing, beside)
    sibling = {"band": chip * 2 + 1 - core}

    def on_chip(c):
        return {"band": c * 2 + core}

    def owner(d):
        return {"lev": d}

    def place(c):
        return c // per_class, pl.ds(c % per_class * chunk, chunk)

    count = y.shape[0]
    halves = groups // 2

    def sample(g, part):
        u, p = g // count, g % count
        kind = 2 if part else u % 2
        return pltpu.make_async_copy(y.at[p, kind], samples.at[g % 2, part], sample_sem.at[g % 2, part])

    def fetch(g):
        sample(g, 0).start()

        @pl.when(g // count % 2 == 0)
        def _():
            sample(g, 1).start()

    def transform(g):
        u, p = g // count, g % count

        @pl.when(g + 1 < 3 * count)
        def _():
            fetch(g + 1)

        def fine(step, l):
            return jnp.broadcast_to(near[p, l, step : step + 1, :], (owners, near.shape[-1])).astype(BF16)

        fill_table(table, halves, owners, lambda k: far[p, u, k], fine)
        keep = functools.partial(keep_wave, total, pl.ds(p, owners, stride=8), fields)
        sample(g, 0).wait()

        @pl.when(u == 1)
        def _():
            waves = transform_waves(table, samples[g % 2, 0], 1, halves, owners)
            for step, (ca, sa, da, ta) in enumerate(waves):
                keep(halves + step, ca, -sa)
                keep(halves - 1 - step, da, -ta)

        @pl.when(u != 1)
        def _():
            sample(g, 1).wait()
            sign = (1 - u).astype(F32)
            rows = samples[g % 2].reshape(4 * fields, samples.shape[-1])
            waves = iter(transform_waves(table, rows, 2, halves, owners))
            for step, ((ca, sa, da, ta), (cb, sb, db, tb)) in enumerate(zip(waves, waves)):
                keep(halves + step, ca - sign * sb, -(sa + sign * cb))
                keep(halves - 1 - step, da - sign * tb, -(ta + sign * db))

        @pl.when(p == count - 1)
        def _():
            def store(t, s, value):
                folded[u + 1, :, t, s] = value

            pack_waves(total, groups, owners, pairs, fields, store)

    def transform_part(q):
        u, i = q // per_class, q % per_class

        def one(p, carry):
            transform(u * count + p)
            return carry

        lax.fori_loop(i * count // per_class, (i + 1) * count // per_class, one, 0)

    fetch(0)
    factors = [
        pltpu.make_async_copy(source, target, factor_sem.at[i])
        for i, (source, target) in enumerate(((first_class, folded.at[0]), (far_hbm, far), (near_hbm, near)))
    ]
    for factor in factors:
        factor.start()
    barrier = pltpu.get_barrier_semaphore()
    for j in range(1, owners):
        pl.semaphore_signal(barrier, inc=1, device_id=owner((lev + j) % owners), device_id_type=MESH)
    for device in (sibling, on_chip(beside), on_chip(facing)):
        pl.semaphore_signal(barrier, inc=1, device_id=device, device_id_type=MESH)
    pl.semaphore_wait(barrier, owners + 2)

    def to_owner(c, d):
        u, t = place(c)
        return pltpu.make_async_remote_copy(
            src_ref=folded.at[u, d, t],
            dst_ref=inbox.at[c, lev],
            send_sem=send_sem.at[c, d],
            recv_sem=recv_sem.at[c, lev],
            device_id=owner(d),
            device_id_type=MESH,
        )

    def from_owner(c, d):
        u, t = place(c)
        return pltpu.make_async_remote_copy(
            src_ref=folded.at[u, d, t],
            dst_ref=inbox.at[c, d],
            send_sem=send_sem.at[c, d],
            recv_sem=recv_sem.at[c, d],
            device_id=owner(d),
            device_id_type=MESH,
        )

    def own(c):
        u, t = place(c)
        return pltpu.make_async_copy(folded.at[u, lev, t], inbox.at[c, lev], recv_sem.at[c, lev])

    def weight(c):
        u, t = place(c)
        return pltpu.make_async_copy(legendre.at[t, u], weights.at[c % (ahead + 1)], weight_sem.at[c])

    def across(c):
        return pltpu.make_async_remote_copy(
            src_ref=partial.at[c % (2 + 2 * gap), 1 - core],
            dst_ref=from_core.at[c],
            send_sem=core_send.at[c],
            recv_sem=core_recv.at[c],
            device_id=sibling,
            device_id_type=MESH,
        )

    def first_step(c, v):
        return pltpu.make_async_remote_copy(
            src_ref=first_out.at[c % (gap + 1), v],
            dst_ref=from_first.at[c, v],
            send_sem=first_send.at[c, v],
            recv_sem=first_recv.at[c, v],
            device_id=on_chip(first[v]),
            device_id_type=MESH,
        )

    def second_step(c, v):
        return pltpu.make_async_remote_copy(
            src_ref=second_out.at[c % (gap + 1), v],
            dst_ref=from_second.at[c, v],
            send_sem=second_send.at[c, v],
            recv_sem=second_recv.at[c, v],
            device_id=on_chip(second[v]),
            device_id_type=MESH,
        )

    def result(c):
        u, t = place(c)
        return pltpu.make_async_copy(staged.at[c % 2], out.at[t, u], out_sem.at[c])

    def launch(c):
        own(c).start()
        weight(c).start()

        def one(j, carry):
            to_owner(c, (lev + j) % owners).start()
            return carry

        lax.fori_loop(1, owners, one, 0)

    def sums(c):
        own(c).wait()
        weight(c).wait()

        def one(j, carry):
            from_owner(c, (lev + j) % owners).wait_recv()
            to_owner(c, (lev + j) % owners).wait_send()
            return carry

        lax.fori_loop(1, owners, one, 0)

        def wave(t, carry):
            for s in range(2):
                f = inbox[c, :, t, s].astype(F32).reshape(owners, 2, pairs, fields)
                part = jnp.concatenate(
                    [f[:, r].reshape(owners * pairs, fields) for r in range(2)], axis=1
                ).astype(BF16)
                total = lax.dot_general(
                    part, weights[c % (ahead + 1), t, s], (((0,), (0,)), ((), ())), preferred_element_type=F32
                ).astype(BF16)
                for r in range(2):
                    for b in range(8):
                        at = r * fields + b * block
                        partial[c % (2 + 2 * gap), b % 2, b // 2, 4 * t + 2 * s + r] = total[at : at + block]
            return carry

        lax.fori_loop(0, chunk, wave, 0)
        across(c).start()

    def parts(c, v, row, target):
        at = pl.ds(v * half + row, ROWS)
        return partial[c % (2 + 2 * gap), core, target, at].astype(F32) + from_core[c, target, at].astype(F32)

    def rows(body):
        def one(i, carry):
            body(i * ROWS)
            return carry

        lax.fori_loop(0, half // ROWS, one, 0)

    def first_stage(c):
        across(c).wait()
        for v in range(2):

            def add(row):
                for w, target in enumerate((first[v], opposite)):
                    first_out[c % (gap + 1), v, w, pl.ds(row, ROWS)] = parts(c, v, row, target).astype(BF16)

            rows(add)
            first_step(c, v).start()

    def second_stage(c):
        for v in range(2):
            first_step(c, v).wait()

            def add(row):
                at = pl.ds(row, ROWS)
                both = parts(c, v, row, second[v]) + from_first[c, v, 1, at].astype(F32)
                second_out[c % (gap + 1), v, at] = both.astype(BF16)

            rows(add)
            second_step(c, v).start()

    def last_stage(c):
        @pl.when(c >= 2)
        def _():
            result(c - 2).wait()

        for v in range(2):
            second_step(c, v).wait()

            def add(row):
                at = pl.ds(row, ROWS)
                both = parts(c, v, row, chip) + from_first[c, v, 0, at].astype(F32) + from_second[c, v, at].astype(F32)
                for i in range(ROWS // 4):
                    staged[c % 2, v * (chunk // 2) + row // 4 + i] = both[4 * i : 4 * i + 4]

            rows(add)
        result(c).start()

    factors[0].wait()
    for c in range(ahead):
        launch(c)
    factors[1].wait()
    factors[2].wait()
    for q in range(ahead - 1):
        transform_part(q)

    def turn(c, carry):
        @pl.when(c + ahead - 1 < 3 * per_class)
        def _():
            transform_part(c + ahead - 1)

        @pl.when(c + ahead < chunks)
        def _():
            launch(c + ahead)

        @pl.when(c < chunks)
        def _():
            sums(c)

        @pl.when((c >= 1) & (c <= chunks))
        def _():
            first_stage(c - 1)

        @pl.when((c >= 1 + gap) & (c <= chunks + gap))
        def _():
            second_stage(c - 1 - gap)

        @pl.when(c >= 1 + 2 * gap)
        def _():
            last_stage(c - 1 - 2 * gap)

        return carry

    lax.fori_loop(0, chunks + 1 + 2 * gap, turn, 0)
    result(chunks - 2).wait()
    result(chunks - 1).wait()


def exchange(y, coarse, fine, first_class, legendre, chunk, ahead, gap):
    count, _, columns, width = y.shape
    owners, fields, both = coarse.shape[3], columns // 2, 2 * count
    groups, _, _, latitudes, degrees = legendre.shape
    chunks = 4 * groups // chunk
    half = 2 * chunk
    block = fields // 8
    dma = pltpu.SemaphoreType.DMA
    anywhere = pl.BlockSpec(memory_space=pl.ANY)
    return pl.pallas_call(
        functools.partial(exchange_kernel, chunk, ahead, gap),
        out_shape=jax.ShapeDtypeStruct((groups, 4, 4, block, degrees), F32),
        in_specs=[anywhere] * 5,
        out_specs=anywhere,
        scratch_shapes=[
            pltpu.VMEM(fine.shape, F32),
            pltpu.VMEM(coarse.shape, BF16),
            pltpu.VMEM((2, 2, columns, width), BF16),
            pltpu.VMEM((2 * groups * owners, width), BF16),
            pltpu.VMEM((4 * groups, owners * count, fields), F32),
            pltpu.VMEM((4, owners, groups, 2, both, fields), BF16),
            pltpu.VMEM((chunks, owners, chunk, 2, both, fields), BF16),
            pltpu.VMEM((ahead + 1, chunk, 2, latitudes, degrees), BF16),
            pltpu.VMEM((2 + 2 * gap, 2, 4, 2 * half, block, degrees), BF16),
            pltpu.VMEM((chunks, 4, 2 * half, block, degrees), BF16),
            pltpu.VMEM((gap + 1, 2, 2, half, block, degrees), BF16),
            pltpu.VMEM((chunks, 2, 2, half, block, degrees), BF16),
            pltpu.VMEM((gap + 1, 2, half, block, degrees), BF16),
            pltpu.VMEM((chunks, 2, half, block, degrees), BF16),
            pltpu.VMEM((2, chunk, 4, block, degrees), F32),
            dma((3,)),
            dma((2, 2)),
            dma((chunks, owners)),
            dma((chunks, owners)),
            dma((chunks,)),
            dma((chunks,)),
            dma((chunks,)),
            dma((chunks, 2)),
            dma((chunks, 2)),
            dma((chunks, 2)),
            dma((chunks, 2)),
            dma((chunks,)),
        ],
        compiler_params=pltpu.CompilerParams(
            collective_id=0, has_side_effects=True, vmem_limit_bytes=60 * 2**20
        ),
    )(coarse, fine, first_class, y, legendre)


CHUNK = 2
AHEAD = 3
GAP = 2


def on_device(owners, grid_values, lon_counts, legendre):
    owned = legendre.shape[0]
    y, coarse, fine, first_class = prepare(grid_values, lon_counts, owners, owned)
    by_class = legendre.reshape(owned // 4, 4, *legendre.shape[1:])
    spectra = exchange(y, coarse, fine, first_class, by_class, CHUNK, AHEAD, GAP)
    return spectra.reshape(owned, 2, 2, *spectra.shape[3:])


def solution(mesh):
    return jax.shard_map(
        functools.partial(on_device, mesh.shape["lev"]),
        mesh=mesh,
        in_specs=(
            P(("band", "lev"), None, None, None),
            P(("band", "lev")),
            P("lev", None, "band", None),
        ),
        out_specs=P("lev", None, None, "band", None),
        check_vma=False,
    )
```

```python
import functools

import jax
import jax.numpy as jnp
from jax import lax
from jax.experimental import pallas as pl
from jax.experimental.pallas import tpu as pltpu
from jax.sharding import PartitionSpec as P

F32 = jnp.float32
BF16 = jnp.bfloat16
COS = (1.0, -19.73920440673828, 64.9390869140625, -85.4496078491211, 60.16310119628906, -25.950063705444336, 6.50340461730957)
SIN = (6.283182621002197, -41.341392517089844, 81.59541320800781, -76.57229614257812, 41.17121124267578, -12.217327117919922)
LANES = 128
ROWS = 4
MESH = pl.DeviceIdType.MESH


def poly(coefs, z):
    out = jnp.full_like(z, coefs[-1])
    for coef in coefs[-2::-1]:
        out = out * z + coef
    return out


def cos_sin(products, count, inverse):
    turns = jnp.floor(products * inverse + 0.5)
    t = (products - turns * count) * inverse
    z = t * t
    return poly(COS, z), t * poly(SIN, z)


def fill_table(table, halves, owners, coarse, fine):
    for step in range(halves):
        for j, (k, l) in enumerate(((0, 0), (1, 0), (0, 1), (1, 1))):
            table[pl.ds((4 * step + j) * owners, owners), :] = coarse(k) * fine(step, l)


def transform_waves(table, rows, parts, halves, owners):
    sums = lax.dot_general(table[...], rows, (((1,), (1,)), ((), ())), preferred_element_type=F32)
    width = rows.shape[0] // parts
    found = []
    for step in range(halves):
        for part in range(parts):
            at = slice(part * width, (part + 1) * width)
            cc, sc, cs, ss = (sums[(4 * step + j) * owners : (4 * step + j + 1) * owners, at] for j in range(4))
            found.append((cc - ss, sc + cs, cc + ss, sc - cs))
    return found


def keep_wave(total, spot, fields, t, real, imag):
    for r, value in enumerate((real, imag)):
        for s in range(2):
            total[4 * t + 2 * r + s, spot, :] = value[:, s * fields : (s + 1) * fields]


def pack_waves(total, groups, owners, pairs, fields, store):
    def pack(t, carry):
        for s in range(2):
            real = total[4 * t + s].reshape(owners, pairs, fields)
            imag = total[4 * t + 2 + s].reshape(owners, pairs, fields)
            store(t, s, jnp.concatenate([real, imag], axis=1).astype(BF16))
        return carry

    lax.fori_loop(0, groups, pack, 0)


def prepare_kernel(owners, owned, counts_ref, x_ref, y_ref, coarse_ref, fine_ref, folded_ref, sum_ref, table, total):
    pair = pl.program_id(0)
    count = counts_ref[pair]
    quarter = lax.shift_right_logical(count, 2)
    fields, points = x_ref.shape[1:]
    width = points // 4
    tiles = width // LANES
    last = points - width - LANES
    rows = 16
    lane = lax.broadcasted_iota(jnp.int32, (rows, LANES), 1)
    starts, shifts = [], []
    for k in range(4):
        start = jnp.minimum(quarter * k // LANES * LANES, last)
        starts.append(start)
        shifts.append(quarter * k - start)

    def fold(step, carry):
        row = pl.ds(pl.multiple_of(step * rows, rows), rows)
        keeps = [lane < LANES - shifts[k] for k in range(4)]

        def turned(k, h, i):
            v = x_ref[h, row, pl.ds(pl.multiple_of(starts[k] + i * LANES, LANES), LANES)]
            return pltpu.roll(v, (LANES - shifts[k]) & (LANES - 1), 1) if k else v

        before = {(k, h): turned(k, h, 0) for k in range(1, 4) for h in range(2)}
        for i in range(tiles):
            at = pl.ds(i * LANES, LANES)
            quarters = []
            for k in range(4):
                both = []
                for h in range(2):
                    if k:
                        after = turned(k, h, i + 1)
                        v = jnp.where(keeps[k], before[k, h], after)
                        before[k, h] = after
                    else:
                        v = turned(k, h, i)
                    both.append(v.astype(F32))
                quarters.append((both[0] + both[1], both[0] - both[1]))
            inside = lane + i * LANES < quarter
            for s in range(2):
                to = pl.ds(pl.multiple_of(step * rows + s * fields, rows), rows)
                x0, x1, x2, x3 = (quarters[k][s] for k in range(4))
                even, odd = x0 + x2, x1 + x3
                for kind, v in enumerate((even + odd, x0 - x2, even - odd, x1 - x3)):
                    if (i + 1) * LANES > points // 8:
                        v = jnp.where(inside, v, 0.0)
                    if kind:
                        y_ref[kind - 1, to, at] = v.astype(BF16)
                    else:
                        sum_ref[to, at] = v.astype(BF16)
        return carry

    lax.fori_loop(0, fields // rows, fold, 0, unroll=2)

    n = count.astype(F32)
    inverse = 1.0 / jnp.full((16, width), n, F32)
    groups = owned // 4
    middle = 2 * groups - 2
    place = lax.broadcasted_iota(jnp.int32, (16, width), 1).astype(F32)
    row = lax.broadcasted_iota(jnp.int32, (16, width), 0).astype(F32)
    rates = jnp.where(row < 8, 4 * row + 2, row + float(middle - 8))
    near_cos, near_sin = cos_sin(place * rates, n, inverse)
    fine_ref[0] = near_cos[:8]
    fine_ref[1] = near_sin[:8]
    owner_cos, owner_sin = cos_sin(place * (row * float(owned)), n, inverse)
    owner_cos, owner_sin = owner_cos * inverse, owner_sin * inverse
    for u in range(4):
        c, s = near_cos[8 + u : 9 + u], near_sin[8 + u : 9 + u]
        far = (owner_cos * c - owner_sin * s).astype(BF16), (owner_sin * c + owner_cos * s).astype(BF16)
        if u:
            coarse_ref[u - 1, 0], coarse_ref[u - 1, 1] = far
        else:
            halves = groups // 2
            near = near_cos, near_sin

            def fine(step, l):
                return jnp.broadcast_to(near[l][step : step + 1], (16, width)).astype(BF16)

            fill_table(table, halves, owners, lambda k: far[k], fine)
            spot = pl.ds(pair, owners, stride=8)
            waves = transform_waves(table, sum_ref[...], 1, halves, owners)
            for step, (ca, sa, da, ta) in enumerate(waves):
                keep_wave(total, spot, fields, halves + step, ca, -sa)
                keep_wave(total, spot, fields, halves - 1 - step, da, -ta)

    @pl.when(pair == pl.num_programs(0) - 1)
    def _():
        def store(t, s, value):
            folded_ref[:, t, s] = value

        pack_waves(total, groups, owners, 8, fields, store)


def prepare(grid_values, lon_counts, owners, owned):
    pairs, _, fields, points = grid_values.shape
    width = points // 4
    groups = owned // 4
    smem = pl.BlockSpec(memory_space=pltpu.SMEM)
    folded = (owners, groups, 2, 2 * pairs, fields)
    return pl.pallas_call(
        functools.partial(prepare_kernel, owners, owned),
        grid=(pairs,),
        out_shape=(
            jax.ShapeDtypeStruct((pairs, 3, 2 * fields, width), BF16),
            jax.ShapeDtypeStruct((pairs, 3, 2, owners, width), BF16),
            jax.ShapeDtypeStruct((pairs, 2, 8, width), F32),
            jax.ShapeDtypeStruct(folded, BF16),
        ),
        in_specs=[smem, pl.BlockSpec((None, 2, fields, points), lambda p: (p, 0, 0, 0))],
        out_specs=(
            pl.BlockSpec((None, 3, 2 * fields, width), lambda p: (p, 0, 0, 0)),
            pl.BlockSpec((None, 3, 2, owners, width), lambda p: (p, 0, 0, 0, 0)),
            pl.BlockSpec((None, 2, 8, width), lambda p: (p, 0, 0, 0)),
            pl.BlockSpec(folded, lambda p: (0, 0, 0, 0, 0)),
        ),
        scratch_shapes=[
            pltpu.VMEM((2 * fields, width), BF16),
            pltpu.VMEM((2 * groups * owners, width), BF16),
            pltpu.VMEM((4 * groups, owners * pairs, fields), F32),
        ],
        compiler_params=pltpu.CompilerParams(vmem_limit_bytes=40 * 2**20),
    )(lon_counts, grid_values)


def exchange_kernel(
    chunk, ahead, gap, far_hbm, near_hbm, first_class, y, legendre, out,
    near, far, samples, table, total, folded, inbox, weights, crossing, partial, from_core, first_out, from_first, second_out, from_second, staged,
    factor_sem, sample_sem, send_sem, recv_sem, weight_sem, core_send, core_recv, first_send, first_recv, second_send, second_recv, out_sem,
):
    _, owners, groups, _, both, fields = folded.shape
    degrees = legendre.shape[-1]
    pairs = both // 2
    per_class = groups // chunk
    chunks = 4 * per_class
    half = 2 * chunk
    block = fields // 8
    band, lev = lax.axis_index("band"), lax.axis_index("lev")
    chip, core = band // 2, band % 2
    beside = chip + 1 - 2 * (chip % 2)
    facing = 3 - chip
    opposite = (chip + 2) % 4
    first, second = (beside, facing), (facing, beside)
    sibling = {"band": chip * 2 + 1 - core}

    def on_chip(c):
        return {"band": c * 2 + core}

    def owner(d):
        return {"lev": d}

    def place(c):
        return c // per_class, pl.ds(c % per_class * chunk, chunk)

    count = y.shape[0]
    halves = groups // 2

    def sample(g, part):
        u, p = g // count, g % count
        kind = 2 if part else u % 2
        return pltpu.make_async_copy(y.at[p, kind], samples.at[part], sample_sem.at[part])

    def fetch(g):
        sample(g, 0).start()

        @pl.when(g // count % 2 == 0)
        def _():
            sample(g, 1).start()

    def transform(g):
        u, p = g // count, g % count

        fetch(g)

        def fine(step, l):
            return jnp.broadcast_to(near[p, l, step : step + 1, :], (owners, near.shape[-1])).astype(BF16)

        fill_table(table, halves, owners, lambda k: far[p, u, k], fine)
        keep = functools.partial(keep_wave, total, pl.ds(p, owners, stride=8), fields)
        sample(g, 0).wait()

        @pl.when(u == 1)
        def _():
            waves = transform_waves(table, samples[0], 1, halves, owners)
            for step, (ca, sa, da, ta) in enumerate(waves):
                keep(halves + step, ca, -sa)
                keep(halves - 1 - step, da, -ta)

        @pl.when(u != 1)
        def _():
            sample(g, 1).wait()
            sign = (1 - u).astype(F32)
            rows = samples[...].reshape(4 * fields, samples.shape[-1])
            waves = iter(transform_waves(table, rows, 2, halves, owners))
            for step, ((ca, sa, da, ta), (cb, sb, db, tb)) in enumerate(zip(waves, waves)):
                keep(halves + step, ca - sign * sb, -(sa + sign * cb))
                keep(halves - 1 - step, da - sign * tb, -(ta + sign * db))

        @pl.when(p == count - 1)
        def _():
            def store(t, s, value):
                folded[(u + 1) % 2, :, t, s] = value

            pack_waves(total, groups, owners, pairs, fields, store)

    def transform_part(q):
        u, i = q // per_class, q % per_class

        def one(p, carry):
            transform(u * count + p)
            return carry

        lax.fori_loop(i * count // per_class, (i + 1) * count // per_class, one, 0)

    factors = [
        pltpu.make_async_copy(source, target, factor_sem.at[i])
        for i, (source, target) in enumerate(((first_class, folded.at[0]), (far_hbm, far), (near_hbm, near)))
    ]
    for factor in factors:
        factor.start()
    barrier = pltpu.get_barrier_semaphore()
    for j in range(1, owners):
        pl.semaphore_signal(barrier, inc=1, device_id=owner((lev + j) % owners), device_id_type=MESH)
    for device in (sibling, on_chip(beside), on_chip(facing)):
        pl.semaphore_signal(barrier, inc=1, device_id=device, device_id_type=MESH)
    pl.semaphore_wait(barrier, owners + 2)

    def to_owner(c, d):
        u, t = place(c)
        return pltpu.make_async_remote_copy(
            src_ref=folded.at[u % 2, d, t],
            dst_ref=inbox.at[c, lev],
            send_sem=send_sem.at[c, d],
            recv_sem=recv_sem.at[c, lev],
            device_id=owner(d),
            device_id_type=MESH,
        )

    def from_owner(c, d):
        u, t = place(c)
        return pltpu.make_async_remote_copy(
            src_ref=folded.at[u % 2, d, t],
            dst_ref=inbox.at[c, d],
            send_sem=send_sem.at[c, d],
            recv_sem=recv_sem.at[c, d],
            device_id=owner(d),
            device_id_type=MESH,
        )

    def own(c):
        u, t = place(c)
        return pltpu.make_async_copy(folded.at[u % 2, lev, t], inbox.at[c, lev], recv_sem.at[c, lev])

    def weight(c):
        u, t = place(c)
        return pltpu.make_async_copy(legendre.at[t, u], weights.at[c % 2], weight_sem.at[c])

    def across(c):
        return pltpu.make_async_remote_copy(
            src_ref=crossing.at[c % 2],
            dst_ref=from_core.at[c],
            send_sem=core_send.at[c],
            recv_sem=core_recv.at[c],
            device_id=sibling,
            device_id_type=MESH,
        )

    def first_step(c, v):
        return pltpu.make_async_remote_copy(
            src_ref=first_out.at[c % (gap + 1), v],
            dst_ref=from_first.at[c, v],
            send_sem=first_send.at[c, v],
            recv_sem=first_recv.at[c, v],
            device_id=on_chip(first[v]),
            device_id_type=MESH,
        )

    def second_step(c, v):
        return pltpu.make_async_remote_copy(
            src_ref=second_out.at[c % (gap + 1), v],
            dst_ref=from_second.at[c, v],
            send_sem=second_send.at[c, v],
            recv_sem=second_recv.at[c, v],
            device_id=on_chip(second[v]),
            device_id_type=MESH,
        )

    def result(c):
        u, t = place(c)
        return pltpu.make_async_copy(staged.at[c % 2], out.at[t, u], out_sem.at[c])

    def launch(c):
        own(c).start()

        def one(j, carry):
            to_owner(c, (lev + j) % owners).start()
            return carry

        lax.fori_loop(1, owners, one, 0)

    def sums(c):
        own(c).wait()
        weight(c).wait()

        def one(j, carry):
            from_owner(c, (lev + j) % owners).wait_recv()
            to_owner(c, (lev + j) % owners).wait_send()
            return carry

        lax.fori_loop(1, owners, one, 0)

        def wave(t, carry):
            for s in range(2):
                f = inbox[c, :, t, s].astype(F32).reshape(owners, 2, pairs, fields)
                part = jnp.concatenate(
                    [f[:, r].reshape(owners * pairs, fields) for r in range(2)], axis=1
                ).astype(BF16)
                total = lax.dot_general(
                    part, weights[c % 2, t, s], (((0,), (0,)), ((), ())), preferred_element_type=F32
                ).astype(BF16)
                for r in range(2):
                    for b in range(4):
                        at = r * fields + 2 * b * block
                        even, odd = total[at : at + block], total[at + block : at + 2 * block]
                        partial[c % (2 + 2 * gap), b, 4 * t + 2 * s + r] = jnp.where(core == 0, even, odd)
                        crossing[c % 2, b, 4 * t + 2 * s + r] = jnp.where(core == 0, odd, even)
            return carry

        lax.fori_loop(0, chunk, wave, 0)
        across(c).start()

    def parts(c, v, row, target):
        at = pl.ds(v * half + row, ROWS)
        return partial[c % (2 + 2 * gap), target, at].astype(F32) + from_core[c, target, at].astype(F32)

    def rows(body):
        def one(i, carry):
            body(i * ROWS)
            return carry

        lax.fori_loop(0, half // ROWS, one, 0)

    def first_stage(c):
        across(c).wait()
        for v in range(2):

            def add(row):
                for w, target in enumerate((first[v], opposite)):
                    first_out[c % (gap + 1), v, w, pl.ds(row, ROWS)] = parts(c, v, row, target).astype(BF16)

            rows(add)
            first_step(c, v).start()

    def second_stage(c):
        for v in range(2):
            first_step(c, v).wait()

            def add(row):
                at = pl.ds(row, ROWS)
                both = parts(c, v, row, second[v]) + from_first[c, v, 1, at].astype(F32)
                second_out[c % (gap + 1), v, at] = both.astype(BF16)

            rows(add)
            second_step(c, v).start()

    def last_stage(c):
        @pl.when(c >= 2)
        def _():
            result(c - 2).wait()

        for v in range(2):
            second_step(c, v).wait()

            def add(row):
                at = pl.ds(row, ROWS)
                both = parts(c, v, row, chip) + from_first[c, v, 0, at].astype(F32) + from_second[c, v, at].astype(F32)
                for i in range(ROWS // 4):
                    staged[c % 2, v * (chunk // 2) + row // 4 + i] = both[4 * i : 4 * i + 4]

            rows(add)
        result(c).start()

    factors[0].wait()
    for c in range(ahead):
        launch(c)
    factors[1].wait()
    factors[2].wait()
    for q in range(ahead - 1):
        transform_part(q)

    weight(0).start()

    def turn(c, carry):
        @pl.when(c + 1 < chunks)
        def _():
            weight(c + 1).start()

        @pl.when(c + ahead - 1 < 3 * per_class)
        def _():
            transform_part(c + ahead - 1)

        @pl.when(c + ahead < chunks)
        def _():
            launch(c + ahead)

        @pl.when(c < chunks)
        def _():
            sums(c)

        @pl.when((c >= 1) & (c <= chunks))
        def _():
            first_stage(c - 1)

        @pl.when((c >= 1 + gap) & (c <= chunks + gap))
        def _():
            second_stage(c - 1 - gap)

        @pl.when(c >= 1 + 2 * gap)
        def _():
            last_stage(c - 1 - 2 * gap)

        return carry

    lax.fori_loop(0, chunks + 1 + 2 * gap, turn, 0)
    result(chunks - 2).wait()
    result(chunks - 1).wait()


def exchange(y, coarse, fine, first_class, legendre, chunk, ahead, gap):
    count, _, columns, width = y.shape
    owners, fields, both = coarse.shape[3], columns // 2, 2 * count
    groups, _, _, latitudes, degrees = legendre.shape
    chunks = 4 * groups // chunk
    half = 2 * chunk
    block = fields // 8
    dma = pltpu.SemaphoreType.DMA
    anywhere = pl.BlockSpec(memory_space=pl.ANY)
    return pl.pallas_call(
        functools.partial(exchange_kernel, chunk, ahead, gap),
        out_shape=jax.ShapeDtypeStruct((groups, 4, 4, block, degrees), F32),
        in_specs=[anywhere] * 5,
        out_specs=anywhere,
        scratch_shapes=[
            pltpu.VMEM(fine.shape, F32),
            pltpu.VMEM(coarse.shape, BF16),
            pltpu.VMEM((2, columns, width), BF16),
            pltpu.VMEM((2 * groups * owners, width), BF16),
            pltpu.VMEM((4 * groups, owners * count, fields), F32),
            pltpu.VMEM((2, owners, groups, 2, both, fields), BF16),
            pltpu.VMEM((chunks, owners, chunk, 2, both, fields), BF16),
            pltpu.VMEM((2, chunk, 2, latitudes, degrees), BF16),
            pltpu.VMEM((2, 4, 2 * half, block, degrees), BF16),
            pltpu.VMEM((2 + 2 * gap, 4, 2 * half, block, degrees), BF16),
            pltpu.VMEM((chunks, 4, 2 * half, block, degrees), BF16),
            pltpu.VMEM((gap + 1, 2, 2, half, block, degrees), BF16),
            pltpu.VMEM((chunks, 2, 2, half, block, degrees), BF16),
            pltpu.VMEM((gap + 1, 2, half, block, degrees), BF16),
            pltpu.VMEM((chunks, 2, half, block, degrees), BF16),
            pltpu.VMEM((2, chunk, 4, block, degrees), F32),
            dma((3,)),
            dma((2,)),
            dma((chunks, owners)),
            dma((chunks, owners)),
            dma((chunks,)),
            dma((chunks,)),
            dma((chunks,)),
            dma((chunks, 2)),
            dma((chunks, 2)),
            dma((chunks, 2)),
            dma((chunks, 2)),
            dma((chunks,)),
        ],
        compiler_params=pltpu.CompilerParams(
            collective_id=0, has_side_effects=True, vmem_limit_bytes=37 * 2**20
        ),
    )(coarse, fine, first_class, y, legendre)


CHUNK = 2
AHEAD = 3
GAP = 2


def on_device(owners, grid_values, lon_counts, legendre):
    owned = legendre.shape[0]
    y, coarse, fine, first_class = prepare(grid_values, lon_counts, owners, owned)
    by_class = legendre.reshape(owned // 4, 4, *legendre.shape[1:])
    spectra = exchange(y, coarse, fine, first_class, by_class, CHUNK, AHEAD, GAP)
    return spectra.reshape(owned, 2, 2, *spectra.shape[3:])


def solution(mesh):
    return jax.shard_map(
        functools.partial(on_device, mesh.shape["lev"]),
        mesh=mesh,
        in_specs=(
            P(("band", "lev"), None, None, None),
            P(("band", "lev")),
            P("lev", None, "band", None),
        ),
        out_specs=P("lev", None, None, "band", None),
        check_vma=False,
    )
```

```python
import functools

import jax
import jax.numpy as jnp
from jax import lax
from jax.experimental import pallas as pl
from jax.experimental.pallas import tpu as pltpu
from jax.sharding import PartitionSpec as P

F32 = jnp.float32
BF16 = jnp.bfloat16
COS = (1.0, -19.73920440673828, 64.9390869140625, -85.4496078491211, 60.16310119628906, -25.950063705444336, 6.50340461730957)
SIN = (6.283182621002197, -41.341392517089844, 81.59541320800781, -76.57229614257812, 41.17121124267578, -12.217327117919922)
LANES = 128
ROWS = 4
TOGETHER = 2
MESH = pl.DeviceIdType.MESH


def poly(coefs, z):
    out = jnp.full_like(z, coefs[-1])
    for coef in coefs[-2::-1]:
        out = out * z + coef
    return out


def cos_sin(products, count, inverse):
    turns = jnp.floor(products * inverse + 0.5)
    t = (products - turns * count) * inverse
    z = t * t
    return poly(COS, z), t * poly(SIN, z)


def fill_table(table, halves, owners, coarse, fine):
    for step in range(halves):
        for j, (k, l) in enumerate(((0, 0), (1, 0), (0, 1), (1, 1))):
            table[pl.ds((4 * step + j) * owners, owners), :] = coarse(k) * fine(step, l)


def transform_waves(table, rows, parts, halves, owners):
    sums = lax.dot_general(table[...], rows, (((1,), (1,)), ((), ())), preferred_element_type=F32)
    width = rows.shape[0] // parts
    found = []
    for step in range(halves):
        for part in range(parts):
            at = slice(part * width, (part + 1) * width)
            cc, sc, cs, ss = (sums[(4 * step + j) * owners : (4 * step + j + 1) * owners, at] for j in range(4))
            found.append((cc - ss, sc + cs, cc + ss, sc - cs))
    return found


def keep_wave(total, spot, fields, t, real, imag):
    for r, value in enumerate((real, imag)):
        for s in range(2):
            total[4 * t + 2 * r + s, spot, :] = value[:, s * fields : (s + 1) * fields]


def pack_waves(total, groups, owners, pairs, fields, store):
    def pack(t, carry):
        for s in range(2):
            real = total[4 * t + s].reshape(owners, pairs, fields)
            imag = total[4 * t + 2 + s].reshape(owners, pairs, fields)
            store(t, s, jnp.concatenate([real, imag], axis=1).astype(BF16))
        return carry

    lax.fori_loop(0, groups, pack, 0)


def prepare_kernel(owned, counts_ref, x_ref, y_ref, coarse_ref, fine_ref, folded_ref, sum_ref, table, total):
    together = x_ref.shape[0]
    for i in range(together):
        refs = (ref.at[i] for ref in (x_ref, y_ref, coarse_ref, fine_ref, sum_ref, table))
        prepare_pair(pl.program_id(0) * together + i, owned, counts_ref, *refs, total)

    @pl.when(pl.program_id(0) == pl.num_programs(0) - 1)
    def _():
        owners, groups, _, both, fields = folded_ref.shape

        def store(t, s, value):
            folded_ref[:, t, s] = value

        pack_waves(total, groups, owners, both // 2, fields, store)


def prepare_pair(pair, owned, counts_ref, x_ref, y_ref, coarse_ref, fine_ref, sum_ref, table, total):
    owners = coarse_ref.shape[2]
    count = counts_ref[pair]
    quarter = lax.shift_right_logical(count, 2)
    fields, points = x_ref.shape[1:]
    width = points // 4
    tiles = width // LANES
    last = points - width - LANES
    rows = 16
    lane = lax.broadcasted_iota(jnp.int32, (rows, LANES), 1)
    starts, shifts = [], []
    for k in range(4):
        start = jnp.minimum(quarter * k // LANES * LANES, last)
        starts.append(start)
        shifts.append(quarter * k - start)

    def fold(step, carry):
        row = pl.ds(pl.multiple_of(step * rows, rows), rows)
        keeps = [lane < LANES - shifts[k] for k in range(4)]

        def turned(k, h, i):
            v = x_ref[h, row, pl.ds(pl.multiple_of(starts[k] + i * LANES, LANES), LANES)]
            return pltpu.roll(v, (LANES - shifts[k]) & (LANES - 1), 1) if k else v

        before = {(k, h): turned(k, h, 0) for k in range(1, 4) for h in range(2)}
        for i in range(tiles):
            at = pl.ds(i * LANES, LANES)
            quarters = []
            for k in range(4):
                both = []
                for h in range(2):
                    if k:
                        after = turned(k, h, i + 1)
                        v = jnp.where(keeps[k], before[k, h], after)
                        before[k, h] = after
                    else:
                        v = turned(k, h, i)
                    both.append(v)
                quarters.append((both[0] + both[1], both[0] - both[1]))
            inside = lane + i * LANES < quarter
            for s in range(2):
                to = pl.ds(pl.multiple_of(step * rows + s * fields, rows), rows)
                x0, x1, x2, x3 = (quarters[k][s] for k in range(4))
                even, odd = x0 + x2, x1 + x3
                for kind, v in enumerate((even + odd, x0 - x2, even - odd, x1 - x3)):
                    if (i + 1) * LANES > points // 8:
                        v = jnp.where(inside, v, jnp.zeros_like(v))
                    if kind:
                        y_ref[kind - 1, to, at] = v.astype(BF16)
                    else:
                        sum_ref[to, at] = v.astype(BF16)
        return carry

    lax.fori_loop(0, fields // rows, fold, 0, unroll=8)

    n = count.astype(F32)
    inverse = 1.0 / jnp.full((16, width), n, F32)
    groups = owned // 4
    middle = 2 * groups - 2
    place = lax.broadcasted_iota(jnp.int32, (16, width), 1).astype(F32)
    row = lax.broadcasted_iota(jnp.int32, (16, width), 0).astype(F32)
    rates = jnp.where(row < 8, 4 * row + 2, row + float(middle - 8))
    near_cos, near_sin = cos_sin(place * rates, n, inverse)
    fine_ref[0] = near_cos[:8]
    fine_ref[1] = near_sin[:8]
    owner_cos, owner_sin = cos_sin(place * (row * float(owned)), n, inverse)
    owner_cos, owner_sin = owner_cos * inverse, owner_sin * inverse
    for u in range(4):
        c, s = near_cos[8 + u : 9 + u], near_sin[8 + u : 9 + u]
        far = (owner_cos * c - owner_sin * s).astype(BF16), (owner_sin * c + owner_cos * s).astype(BF16)
        if u:
            coarse_ref[u - 1, 0], coarse_ref[u - 1, 1] = far
        else:
            halves = groups // 2
            near = near_cos, near_sin

            def fine(step, l):
                return jnp.broadcast_to(near[l][step : step + 1], (16, width)).astype(BF16)

            fill_table(table, halves, owners, lambda k: far[k], fine)
            spot = pl.ds(pair, owners, stride=8)
            waves = transform_waves(table, sum_ref[...], 1, halves, owners)
            for step, (ca, sa, da, ta) in enumerate(waves):
                keep_wave(total, spot, fields, halves + step, ca, -sa)
                keep_wave(total, spot, fields, halves - 1 - step, da, -ta)


def prepare(grid_values, lon_counts, owners, owned):
    pairs, _, fields, points = grid_values.shape
    width = points // 4
    groups = owned // 4
    smem = pl.BlockSpec(memory_space=pltpu.SMEM)
    folded = (owners, groups, 2, 2 * pairs, fields)
    return pl.pallas_call(
        functools.partial(prepare_kernel, owned),
        grid=(pairs // TOGETHER,),
        out_shape=(
            jax.ShapeDtypeStruct((pairs, 3, 2 * fields, width), BF16),
            jax.ShapeDtypeStruct((pairs, 3, 2, owners, width), BF16),
            jax.ShapeDtypeStruct((pairs, 2, 8, width), F32),
            jax.ShapeDtypeStruct(folded, BF16),
        ),
        in_specs=[smem, pl.BlockSpec((TOGETHER, 2, fields, points), lambda p: (p, 0, 0, 0))],
        out_specs=(
            pl.BlockSpec((TOGETHER, 3, 2 * fields, width), lambda p: (p, 0, 0, 0)),
            pl.BlockSpec((TOGETHER, 3, 2, owners, width), lambda p: (p, 0, 0, 0, 0)),
            pl.BlockSpec((TOGETHER, 2, 8, width), lambda p: (p, 0, 0, 0)),
            pl.BlockSpec(folded, lambda p: (0, 0, 0, 0, 0)),
        ),
        scratch_shapes=[
            pltpu.VMEM((TOGETHER, 2 * fields, width), BF16),
            pltpu.VMEM((TOGETHER, 2 * groups * owners, width), BF16),
            pltpu.VMEM((4 * groups, owners * pairs, fields), F32),
        ],
        compiler_params=pltpu.CompilerParams(vmem_limit_bytes=40 * 2**20),
    )(lon_counts, grid_values)


def exchange_kernel(
    chunk, ahead, gap, far_hbm, near_hbm, first_class, y, legendre, out,
    near, far, samples, table, total, folded, inbox, weights, crossing, partial, from_core, first_out, from_first, second_out, from_second, staged,
    factor_sem, sample_sem, send_sem, recv_sem, weight_sem, core_send, core_recv, first_send, first_recv, second_send, second_recv, out_sem,
):
    _, owners, groups, _, both, fields = folded.shape
    degrees = legendre.shape[-1]
    pairs = both // 2
    per_class = groups // chunk
    chunks = 4 * per_class
    half = 2 * chunk
    block = fields // 8
    band, lev = lax.axis_index("band"), lax.axis_index("lev")
    chip, core = band // 2, band % 2
    beside = chip + 1 - 2 * (chip % 2)
    facing = 3 - chip
    opposite = (chip + 2) % 4
    first, second = (beside, facing), (facing, beside)
    sibling = {"band": chip * 2 + 1 - core}

    def on_chip(c):
        return {"band": c * 2 + core}

    def owner(d):
        return {"lev": d}

    def place(c):
        return c // per_class, pl.ds(c % per_class * chunk, chunk)

    count = y.shape[0]
    halves = groups // 2

    def sample(g, part):
        u, p = g // count, g % count
        kind = 2 if part else u % 2
        return pltpu.make_async_copy(y.at[p, kind], samples.at[part], sample_sem.at[part])

    def fetch(g):
        sample(g, 0).start()

        @pl.when(g // count % 2 == 0)
        def _():
            sample(g, 1).start()

    def transform(g):
        u, p = g // count, g % count

        fetch(g)

        def fine(step, l):
            return jnp.broadcast_to(near[p, l, step : step + 1, :], (owners, near.shape[-1])).astype(BF16)

        fill_table(table, halves, owners, lambda k: far[p, u, k], fine)
        keep = functools.partial(keep_wave, total, pl.ds(p, owners, stride=8), fields)
        sample(g, 0).wait()

        @pl.when(u == 1)
        def _():
            waves = transform_waves(table, samples[0], 1, halves, owners)
            for step, (ca, sa, da, ta) in enumerate(waves):
                keep(halves + step, ca, -sa)
                keep(halves - 1 - step, da, -ta)

        @pl.when(u != 1)
        def _():
            sample(g, 1).wait()
            sign = (1 - u).astype(F32)
            rows = samples[...].reshape(4 * fields, samples.shape[-1])
            waves = iter(transform_waves(table, rows, 2, halves, owners))
            for step, ((ca, sa, da, ta), (cb, sb, db, tb)) in enumerate(zip(waves, waves)):
                keep(halves + step, ca - sign * sb, -(sa + sign * cb))
                keep(halves - 1 - step, da - sign * tb, -(ta + sign * db))

        @pl.when(p == count - 1)
        def _():
            def store(t, s, value):
                folded[(u + 1) % 2, :, t, s] = value

            pack_waves(total, groups, owners, pairs, fields, store)

    def transform_part(q):
        u, i = q // per_class, q % per_class

        def one(p, carry):
            transform(u * count + p)
            return carry

        lax.fori_loop(i * count // per_class, (i + 1) * count // per_class, one, 0)

    factors = [
        pltpu.make_async_copy(source, target, factor_sem.at[i])
        for i, (source, target) in enumerate(((first_class, folded.at[0]), (far_hbm, far), (near_hbm, near)))
    ]
    for factor in factors:
        factor.start()
    barrier = pltpu.get_barrier_semaphore()
    for j in range(1, owners):
        pl.semaphore_signal(barrier, inc=1, device_id=owner((lev + j) % owners), device_id_type=MESH)
    for device in (sibling, on_chip(beside), on_chip(facing)):
        pl.semaphore_signal(barrier, inc=1, device_id=device, device_id_type=MESH)
    pl.semaphore_wait(barrier, owners + 2)

    def to_owner(c, d, early=False):
        u, t = place(c)
        return pltpu.make_async_remote_copy(
            src_ref=first_class.at[d, t] if early else folded.at[u % 2, d, t],
            dst_ref=inbox.at[c, lev],
            send_sem=send_sem.at[c, d],
            recv_sem=recv_sem.at[c, lev],
            device_id=owner(d),
            device_id_type=MESH,
        )

    def from_owner(c, d):
        u, t = place(c)
        return pltpu.make_async_remote_copy(
            src_ref=folded.at[u % 2, d, t],
            dst_ref=inbox.at[c, d],
            send_sem=send_sem.at[c, d],
            recv_sem=recv_sem.at[c, d],
            device_id=owner(d),
            device_id_type=MESH,
        )

    def own(c, early=False):
        u, t = place(c)
        source = first_class.at[lev, t] if early else folded.at[u % 2, lev, t]
        return pltpu.make_async_copy(source, inbox.at[c, lev], recv_sem.at[c, lev])

    def weight(c):
        u, t = place(c)
        return pltpu.make_async_copy(legendre.at[t, u], weights.at[c % 2], weight_sem.at[c])

    def across(c):
        return pltpu.make_async_remote_copy(
            src_ref=crossing.at[c % 2],
            dst_ref=from_core.at[c],
            send_sem=core_send.at[c],
            recv_sem=core_recv.at[c],
            device_id=sibling,
            device_id_type=MESH,
        )

    def first_step(c, v):
        return pltpu.make_async_remote_copy(
            src_ref=first_out.at[c % (gap + 1), v],
            dst_ref=from_first.at[c, v],
            send_sem=first_send.at[c, v],
            recv_sem=first_recv.at[c, v],
            device_id=on_chip(first[v]),
            device_id_type=MESH,
        )

    def second_step(c, v):
        return pltpu.make_async_remote_copy(
            src_ref=second_out.at[c % (gap + 1), v],
            dst_ref=from_second.at[c, v],
            send_sem=second_send.at[c, v],
            recv_sem=second_recv.at[c, v],
            device_id=on_chip(second[v]),
            device_id_type=MESH,
        )

    def result(c):
        u, t = place(c)
        return pltpu.make_async_copy(staged.at[c % 2], out.at[t, u], out_sem.at[c])

    def launch(c, early=False):
        own(c, early).start()

        def one(j, carry):
            to_owner(c, (lev + j) % owners, early).start()
            return carry

        lax.fori_loop(1, owners, one, 0)

    def sums(c):
        own(c).wait()
        weight(c).wait()

        def one(j, carry):
            from_owner(c, (lev + j) % owners).wait_recv()
            to_owner(c, (lev + j) % owners).wait_send()
            return carry

        lax.fori_loop(1, owners, one, 0)

        def wave(t, carry):
            for s in range(2):
                f = inbox[c, :, t, s].astype(F32).reshape(owners, 2, pairs, fields)
                part = jnp.concatenate(
                    [f[:, r].reshape(owners * pairs, fields) for r in range(2)], axis=1
                ).astype(BF16)
                total = lax.dot_general(
                    part, weights[c % 2, t, s], (((0,), (0,)), ((), ())), preferred_element_type=F32
                ).astype(BF16)
                for r in range(2):
                    for b in range(4):
                        at = r * fields + 2 * b * block
                        even, odd = total[at : at + block], total[at + block : at + 2 * block]
                        partial[c % (2 + 2 * gap), b, 4 * t + 2 * s + r] = jnp.where(core == 0, even, odd)
                        crossing[c % 2, b, 4 * t + 2 * s + r] = jnp.where(core == 0, odd, even)
            return carry

        lax.fori_loop(0, chunk, wave, 0)
        across(c).start()

    def parts(c, v, row, target):
        at = pl.ds(v * half + row, ROWS)
        return partial[c % (2 + 2 * gap), target, at].astype(F32) + from_core[c, target, at].astype(F32)

    def rows(body):
        def one(i, carry):
            body(i * ROWS)
            return carry

        lax.fori_loop(0, half // ROWS, one, 0)

    def first_stage(c):
        across(c).wait()
        for v in range(2):

            def add(row):
                for w, target in enumerate((first[v], opposite)):
                    first_out[c % (gap + 1), v, w, pl.ds(row, ROWS)] = parts(c, v, row, target).astype(BF16)

            rows(add)
            first_step(c, v).start()

    def second_stage(c):
        for v in range(2):
            first_step(c, v).wait()

            def add(row):
                at = pl.ds(row, ROWS)
                both = parts(c, v, row, second[v]) + from_first[c, v, 1, at].astype(F32)
                second_out[c % (gap + 1), v, at] = both.astype(BF16)

            rows(add)
            second_step(c, v).start()

    def last_stage(c):
        @pl.when(c >= 2)
        def _():
            result(c - 2).wait()

        for v in range(2):
            second_step(c, v).wait()

            def add(row):
                at = pl.ds(row, ROWS)
                both = parts(c, v, row, chip) + from_first[c, v, 0, at].astype(F32) + from_second[c, v, at].astype(F32)
                for i in range(ROWS // 4):
                    staged[c % 2, v * (chunk // 2) + row // 4 + i] = both[4 * i : 4 * i + 4]

            rows(add)
        result(c).start()

    weight(0).start()
    for c in range(ahead):
        launch(c, True)
    for factor in factors:
        factor.wait()
    for q in range(ahead - 1):
        transform_part(q)

    def turn(c, carry):
        @pl.when(c + 1 < chunks)
        def _():
            weight(c + 1).start()

        @pl.when(c + ahead - 1 < 3 * per_class)
        def _():
            transform_part(c + ahead - 1)

        @pl.when(c + ahead < chunks)
        def _():
            launch(c + ahead)

        @pl.when((c >= 1) & (c <= chunks))
        def _():
            first_stage(c - 1)

        @pl.when((c >= 1 + gap) & (c <= chunks + gap))
        def _():
            second_stage(c - 1 - gap)

        @pl.when(c >= 1 + 2 * gap)
        def _():
            last_stage(c - 1 - 2 * gap)

        @pl.when(c < chunks)
        def _():
            sums(c)

        return carry

    lax.fori_loop(0, chunks + 1 + 2 * gap, turn, 0)
    result(chunks - 2).wait()
    result(chunks - 1).wait()


def exchange(y, coarse, fine, first_class, legendre, chunk, ahead, gap):
    count, _, columns, width = y.shape
    owners, fields, both = coarse.shape[3], columns // 2, 2 * count
    groups, _, _, latitudes, degrees = legendre.shape
    chunks = 4 * groups // chunk
    half = 2 * chunk
    block = fields // 8
    dma = pltpu.SemaphoreType.DMA
    anywhere = pl.BlockSpec(memory_space=pl.ANY)
    return pl.pallas_call(
        functools.partial(exchange_kernel, chunk, ahead, gap),
        out_shape=jax.ShapeDtypeStruct((groups, 4, 4, block, degrees), F32),
        in_specs=[anywhere] * 5,
        out_specs=anywhere,
        scratch_shapes=[
            pltpu.VMEM(fine.shape, F32),
            pltpu.VMEM(coarse.shape, BF16),
            pltpu.VMEM((2, columns, width), BF16),
            pltpu.VMEM((2 * groups * owners, width), BF16),
            pltpu.VMEM((4 * groups, owners * count, fields), F32),
            pltpu.VMEM((2, owners, groups, 2, both, fields), BF16),
            pltpu.VMEM((chunks, owners, chunk, 2, both, fields), BF16),
            pltpu.VMEM((2, chunk, 2, latitudes, degrees), BF16),
            pltpu.VMEM((2, 4, 2 * half, block, degrees), BF16),
            pltpu.VMEM((2 + 2 * gap, 4, 2 * half, block, degrees), BF16),
            pltpu.VMEM((chunks, 4, 2 * half, block, degrees), BF16),
            pltpu.VMEM((gap + 1, 2, 2, half, block, degrees), BF16),
            pltpu.VMEM((chunks, 2, 2, half, block, degrees), BF16),
            pltpu.VMEM((gap + 1, 2, half, block, degrees), BF16),
            pltpu.VMEM((chunks, 2, half, block, degrees), BF16),
            pltpu.VMEM((2, chunk, 4, block, degrees), F32),
            dma((3,)),
            dma((2,)),
            dma((chunks, owners)),
            dma((chunks, owners)),
            dma((chunks,)),
            dma((chunks,)),
            dma((chunks,)),
            dma((chunks, 2)),
            dma((chunks, 2)),
            dma((chunks, 2)),
            dma((chunks, 2)),
            dma((chunks,)),
        ],
        compiler_params=pltpu.CompilerParams(
            collective_id=0, has_side_effects=True, vmem_limit_bytes=37 * 2**20
        ),
    )(coarse, fine, first_class, y, legendre)


CHUNK = 2
AHEAD = 3
GAP = 2


def on_device(owners, grid_values, lon_counts, legendre):
    owned = legendre.shape[0]
    y, coarse, fine, first_class = prepare(grid_values, lon_counts, owners, owned)
    by_class = legendre.reshape(owned // 4, 4, *legendre.shape[1:])
    spectra = exchange(y, coarse, fine, first_class, by_class, CHUNK, AHEAD, GAP)
    return spectra.reshape(owned, 2, 2, *spectra.shape[3:])


def solution(mesh):
    return jax.shard_map(
        functools.partial(on_device, mesh.shape["lev"]),
        mesh=mesh,
        in_specs=(
            P(("band", "lev"), None, None, None),
            P(("band", "lev")),
            P("lev", None, "band", None),
        ),
        out_specs=P("lev", None, None, "band", None),
        check_vma=False,
    )
```
